128 devices in a mesh: section: 2 (over x_lo), tensor: 16 (over z, y), dp: 4 (over x_hi, core).
Axes of the slice: x: 4 (x_hi: 2, x_lo: 2; x = x_hi * 2 + x_lo), y: 4, z: 4, core: 2. Of those that a mesh axis runs over, the one named last changes fastest.
Arguments:
- teacher_input: bfloat16 [2048, 16384], P(('section', 'dp'), 'tensor'), may hold values from -17 to 17
- teacher_proj: bfloat16 [16384, 16384], P('tensor', ('section', 'dp'))
- teacher_gain: float32 [16384], P(('section', 'dp')), may hold values from 0.25 to 1.75
- projector: bfloat16 [16384, 8192], P(('section', 'dp'), 'tensor'), may hold values from -0.046875 to 0.046875
- student_input: bfloat16 [2048, 8192], P(('section', 'dp'), 'tensor'), may hold values from -19 to 19
- student_gain: float32 [8192], P('tensor'), may hold values from 0.25 to 1.75
- student_weight: bfloat16 [8192, 8192], P(None, 'tensor'), may hold values from -0.0625 to 0.0625
- loss_mask: int32 [2048], P(('section', 'dp')), may hold values 0 or 1
Outputs:
- weight_grad: float32 [8192, 8192], P(('section', 'dp'), 'tensor')
- input_grad: bfloat16 [2048, 8192], P(('section', 'dp'), 'tensor')
The draws below stay inside these ranges and needn't reach their ends.
All inputs are finite; a program needn't handle non-finite values. No bound on the sum of `loss_mask` on one device may be relied on, other than what follows from the above.
Results may differ from the reference program's by a relative error of at most 0.023.
Values may be sent and summed in bfloat16 or wider, within the bound.
No kernel may reach another device: no remote copies, remote signals or barrier semaphores. Data moves between devices by JAX's collectives and lax.ppermute only.
A program may use at most 128 MiB of HBM per device.

```python
import math
import jax
import jax.numpy as jnp
from jax import lax

DT = 16384
DS = 8192
TOKENS = 2048
N_TENSOR = 16


def draw_teacher_input(key, part):
    key = jax.random.fold_in(key, 11)
    base_key, row_key, col_key = jax.random.split(key, 3)
    base = jnp.clip(jax.random.normal(base_key, (TOKENS, DT), jnp.float32), -4.0, 4.0)
    spread = 3.0
    row_scale = jnp.exp(jax.random.uniform(row_key, (TOKENS, 1), jnp.float32, -math.log(spread), math.log(spread)))
    col_scale = jax.random.uniform(col_key, (1, DT), jnp.float32, 0.6, 1.4)
    return (base * row_scale * col_scale).astype(jnp.bfloat16)


def draw_teacher_proj(key, part):
    key = jax.random.fold_in(key, 23)
    base_key, col_key = jax.random.split(key, 2)
    base = jnp.clip(jax.random.normal(base_key, (DT, DT), jnp.float32), -4.0, 4.0)
    rise = 3.0
    low = 0.6
    position = jnp.arange(DT, dtype=jnp.float32)[None, :] / max(DT - 1, 1)
    ramp = low * jnp.exp(math.log(rise) * position)
    rough = jax.random.uniform(col_key, (1, DT), jnp.float32, 0.7, 1.3)
    return (base * ramp * rough / math.sqrt(DT)).astype(jnp.bfloat16)


def draw_student_input(key, part):
    key = jax.random.fold_in(key, 37)
    base_key, row_key, col_key = jax.random.split(key, 3)
    base = jnp.clip(jax.random.normal(base_key, (TOKENS, DS), jnp.float32), -4.0, 4.0)
    spread = 2.0
    row_scale = jnp.exp(jax.random.uniform(row_key, (TOKENS, 1), jnp.float32, -math.log(spread), math.log(spread)))
    position = jnp.arange(DS, dtype=jnp.float32)[None, :] / max(DS - 1, 1)
    ramp = 0.6 * jnp.exp(math.log(3.0) * position)
    rough = jax.random.uniform(col_key, (1, DS), jnp.float32, 0.7, 1.3)
    return (base * row_scale * ramp * rough).astype(jnp.bfloat16)


def plant(array, rng, low, largest):
    longest = array.shape.index(max(array.shape))
    spots = []
    for shift in (0, 1):
        where = [jax.random.randint(jax.random.fold_in(rng, axis), (), 0, length) for axis, length in enumerate(array.shape)]
        where[longest] = (where[longest] + shift) % array.shape[longest]
        spots.append(tuple(where))
    return array.at[spots[0]].set(low).at[spots[1]].set(largest)


def levels(rng, shape, cuts, low, largest):
    loudness = 1.0
    for dim, parts in cuts:
        draws = jax.random.uniform(jax.random.fold_in(jax.random.fold_in(rng, 6), dim), (parts,), jnp.float32, low / len(cuts), largest / len(cuts))
        loudness = loudness * jnp.repeat(jnp.exp(draws), shape[dim] // parts).reshape((-1,) + (1,) * (len(shape) - 1 - dim))
    return loudness


def scatter_about(own_key, dims, scale, limit, pieces=(), kind=jnp.bfloat16):
    gain = levels(own_key, dims, pieces, -0.22, 0.18) if pieces else 1.0
    entries = jax.random.normal(own_key, dims, jnp.float32) * scale * gain
    return jnp.minimum(jnp.maximum(entries, -limit), limit).astype(kind)


def setup_inputs(seed: int = 0) -> dict:
    streams_of = jax.random.split(jax.random.key(seed), 9)
    teacher_input = draw_teacher_input(jax.random.fold_in(streams_of[8], 71), 0)
    teacher_proj = draw_teacher_proj(jax.random.fold_in(streams_of[8], 71), 0)
    teacher_gain = jnp.clip(1.0 + 0.15 * jax.random.normal(streams_of[2], (DT,), jnp.float32), 0.25, 1.75)
    projector = scatter_about(streams_of[3], (DT, DS), DT ** -0.5, 0.046875, ((0, 8), (1, 16)))
    student_input = draw_student_input(jax.random.fold_in(streams_of[8], 71), 0)
    student_gain = jnp.clip(1.0 + 0.15 * jax.random.normal(streams_of[5], (DS,), jnp.float32), 0.25, 1.75)
    student_weight = scatter_about(streams_of[6], (DS, DS), DS ** -0.5, 0.0625, ((1, 16),))
    loss_mask = plant((jax.random.randint(streams_of[7], (TOKENS,), 0, 4) < 3).astype(jnp.int32), jax.random.fold_in(streams_of[7], 1), 0, 1)
    return {"teacher_input": teacher_input, "teacher_proj": teacher_proj, "teacher_gain": teacher_gain, "projector": projector, "student_input": student_input, "student_gain": student_gain, "student_weight": student_weight, "loss_mask": loss_mask}


EPSILON = 1e-05

def reference(teacher_input, teacher_proj, teacher_gain, projector, student_input, student_gain, student_weight, loss_mask):
    block_t = DT // N_TENSOR
    block_s = DS // N_TENSOR

    def teacher_block(total, index):
        begin = (index * block_t).astype(jnp.int32)
        piece = lax.dynamic_slice_in_dim(teacher_input, begin, block_t, 1).astype(jnp.float32)
        weight_rows = lax.dynamic_slice_in_dim(teacher_proj, begin, block_t, 0).astype(jnp.float32)
        term = jnp.dot(piece, weight_rows, precision=lax.Precision.HIGHEST)
        term = lax.optimization_barrier(term.astype(jnp.bfloat16)).astype(jnp.float32)
        return (total + term, None)
    hidden, _ = lax.scan(teacher_block, jnp.zeros((TOKENS, DT), jnp.float32), jnp.arange(N_TENSOR, dtype=jnp.int32))
    teacher_power = lax.optimization_barrier(jnp.sum(hidden * hidden, axis=1))
    normed = (hidden * lax.rsqrt(teacher_power / DT + EPSILON)[:, None] * teacher_gain).astype(jnp.bfloat16)
    target = jnp.dot(normed.astype(jnp.float32), projector.astype(jnp.float32), precision=lax.Precision.HIGHEST).astype(jnp.bfloat16)
    inputs = student_input.astype(jnp.float32)
    inv_scale = lax.rsqrt(lax.optimization_barrier(jnp.sum(inputs * inputs, axis=1)) / DS + EPSILON)
    features = (inputs * inv_scale[:, None] * student_gain).astype(jnp.bfloat16)
    weight_f = student_weight.astype(jnp.float32)
    output = inputs + jnp.dot(features.astype(jnp.float32), weight_f, precision=lax.Precision.HIGHEST)
    error = loss_mask.astype(jnp.float32)[:, None] * (output - target.astype(jnp.float32))
    error_b = error.astype(jnp.bfloat16)
    error_f = error_b.astype(jnp.float32)
    weight_grad = jnp.dot(features.astype(jnp.float32).T, error_f, precision=lax.Precision.HIGHEST)

    def back_block(total, index):
        begin = (index * block_s).astype(jnp.int32)
        err_cols = lax.dynamic_slice_in_dim(error_f, begin, block_s, 1)
        weight_cols = lax.dynamic_slice_in_dim(weight_f, begin, block_s, 1)
        term = jnp.dot(err_cols, weight_cols.T, precision=lax.Precision.HIGHEST)
        term = lax.optimization_barrier(term.astype(jnp.bfloat16)).astype(jnp.float32)
        return (total + term, None)
    feature_grad, _ = lax.scan(back_block, jnp.zeros((TOKENS, DS), jnp.float32), jnp.arange(N_TENSOR, dtype=jnp.int32))
    inner = lax.optimization_barrier(jnp.sum(feature_grad * student_gain * inputs, axis=1))
    input_grad = error + inv_scale[:, None] * student_gain * feature_grad - inputs * (inv_scale ** 3 * inner / DS)[:, None]
    return (weight_grad, input_grad.astype(jnp.bfloat16))
```

```python
import jax
import jax.numpy as jnp
from jax import lax
from jax.experimental import pallas as pl
from jax.experimental.pallas import tpu as pltpu
from jax.sharding import Mesh, PartitionSpec as P

DT = 16384
DS = 8192
EPSILON = 1e-05
F32 = jnp.float32
BF16 = jnp.bfloat16

X = ("section", "xhi")
ZYC = ("z", "y", "core")
HOPS = (0, 2, 3, 1)
FLIP = ((1, 0), (0, 1), (3, 0), (0, 3))
ANYWHERE = pl.BlockSpec(memory_space=pl.ANY)


def dot(a, b):
    return jnp.dot(a, b, preferred_element_type=F32)


def dot_t(a, b):
    return lax.dot_general(a, b, (((1,), (1,)), ((), ())), preferred_element_type=F32)


def first_of(j, core, step):
    return (3 - core if j else core) + step


def swap_zy(value, j, step):
    perm = []
    for z in range(4):
        for y in range(4):
            for core in range(2):
                dz, dy = FLIP[first_of(j, core, step) % 4]
                perm.append(((z * 4 + y) * 2 + core, ((z ^ dz) * 4 + (y ^ dy)) * 2 + core))
    return lax.ppermute(value, ZYC, perm)


def swap_x(value, r):
    return lax.ppermute(value, X, [(j, j ^ r) for j in range(4)])


def swap_core(value):
    return lax.ppermute(value, "core", [(0, 1), (1, 0)])


def split3(value):
    high = value.astype(BF16)
    rest = value - high.astype(F32)
    mid = rest.astype(BF16)
    low = (rest - mid.astype(F32)).astype(BF16)
    return high, mid, low


def call(kernel, grid, scalars, ins, outs, deps=(), scratch=(), moved=0, flops=0):
    n, m = len(ins), len(outs)

    def body(where, *refs):
        kernel(where, *refs[:n], *refs[n + len(deps) :])

    result = pl.pallas_call(
        body,
        grid_spec=pltpu.PrefetchScalarGridSpec(
            num_scalar_prefetch=1,
            grid=(grid,),
            in_specs=[pl.BlockSpec(b, i) for _, b, i in ins] + [ANYWHERE] * len(deps),
            out_specs=[pl.BlockSpec(b, i) for _, b, i in outs],
            scratch_shapes=list(scratch),
        ),
        out_shape=[s for s, _, _ in outs],
        compiler_params=pltpu.CompilerParams(vmem_limit_bytes=16 << 20),
        cost_estimate=pl.CostEstimate(flops=flops, bytes_accessed=moved, transcendentals=0),
    )(scalars, *[a for a, _, _ in ins], *deps)
    return result


def shape(dims, dtype):
    return jax.ShapeDtypeStruct(dims, dtype)


def nothing(*refs):
    pass


def after(values, *deps):
    n = len(values)
    return pl.pallas_call(
        nothing,
        in_specs=[ANYWHERE] * (n + len(deps)),
        out_specs=[ANYWHERE] * n,
        out_shape=[shape(v.shape, v.dtype) for v in values],
        input_output_aliases={i: i for i in range(n)},
        cost_estimate=pl.CostEstimate(flops=0, bytes_accessed=0, transcendentals=0),
    )(*values, *deps)


def target_of(r, where, j):
    dz, dy = 0, 0
    for step in range(4):
        on = (r >> (3 - step)) & 1
        d = first_of(j, where[2], step) & 3
        flip = on * ((d & 2) + 1)
        dz = dz ^ jnp.where(d & 1 == 0, flip, 0)
        dy = dy ^ jnp.where(d & 1 == 1, flip, 0)
    return (where[0] ^ dz) * 4 + (where[1] ^ dy)


def block_of(t, where, j):
    gz, gy = (t >> 2) ^ where[0], (t & 3) ^ where[1]
    r = 0
    for step in range(4):
        d = first_of(j, where[2], step) & 3
        g = jnp.where(d & 1 == 0, gz, gy)
        gray = jnp.where(d & 2 == 0, (g ^ (g >> 1)) & 1, g >> 1)
        r = r | (gray << (3 - step))
    return r


def order_columns(proj, where):
    def kernel(where, a, b, out_a, out_b):
        out_a[...] = a[...]
        out_b[...] = b[...]

    return call(
        kernel,
        16,
        where,
        [(proj, (1024, 128), lambda r, w, j=j: (0, r ^ w[4 + j])) for j in range(2)],
        [(shape((1024, 2048), BF16), (1024, 128), lambda r, w: (0, r)) for j in range(2)],
        moved=4 * proj.size * 2,
    )


def order_projector(projector, gain, where, deps):
    def kernel(where, a, b, gain_a, gain_b, out_a, out_b):
        out_a[...] = (a[...].astype(F32) * gain_a[...]).astype(BF16)
        out_b[...] = (b[...].astype(F32) * gain_b[...]).astype(BF16)

    gain = gain[:, None]
    return call(
        kernel,
        16,
        where,
        [(projector, (128, 512), lambda r, w, j=j: (r ^ w[4 + j], 0)) for j in range(2)]
        + [(gain, (128, 1), lambda r, w, j=j: (r ^ w[4 + j], 0)) for j in range(2)],
        [(shape((2048, 512), BF16), (128, 512), lambda r, w: (r, 0)) for j in range(2)],
        deps=deps,
        moved=4 * projector.size * 2,
    )


def order_rows(weight, where, deps):
    def kernel(where, a, b, out_a, out_b):
        out_a[...] = a[...]
        out_b[...] = b[...]

    return call(
        kernel,
        16,
        where,
        [
            (weight, (256, 512), lambda r, w, j=j: (target_of(r, w, j) * 2 + j, 0))
            for j in range(2)
        ],
        [(shape((4096, 512), BF16), (256, 512), lambda r, w: (r, 0)) for j in range(2)],
        deps=deps,
        moved=2 * weight.size * 2,
    )


def norm_rows(first, second, inv_scale, where, deps):
    def chip_of(g, w):
        k = g >> 2
        hop = jnp.where(k == 0, HOPS[0], jnp.where(k == 1, HOPS[1], jnp.where(k == 2, HOPS[2], HOPS[3])))
        return ((w[3] ^ hop) << 2) | (g & 3)

    def kernel(where, scale, a, b, *outs):
        g = pl.program_id(0)
        for k in range(4):

            @pl.when((g >> 2) == k)
            def _(k=k):
                for j, ref in enumerate((a, b)):
                    rows = ref[:256, :].astype(F32)
                    parts = ref[256:272, :].astype(F32)
                    gain = parts[0:1] + parts[1:2] + parts[2:3]
                    outs[k][:, j * 256 : (j + 1) * 256] = (rows * scale[...] * gain).astype(BF16)

    return call(
        kernel,
        16,
        where,
        [(inv_scale[:, None], (256, 1), lambda g, w: (0, 0))]
        + [
            (v, (272, 256), lambda g, w, j=j: (0, block_of(chip_of(g, w), w, j)))
            for j, v in enumerate((first, second))
        ],
        [
            (
                shape((256, 2048), BF16),
                (256, 512),
                lambda g, w, k=k: (0, jnp.clip(g - 4 * k, 0, 3)),
            )
            for k in range(4)
        ],
        deps=deps,
        moved=4 * first.size * 2,
    )


def forward(features, weight, where, deps):
    def row_of(g, w):
        k = g >> 2
        hop = jnp.where(k == 0, HOPS[0], jnp.where(k == 1, HOPS[1], jnp.where(k == 2, HOPS[2], HOPS[3])))
        return ((w[3] ^ hop) << 2) | (g & 3)

    def kernel(where, a, b, c, d, weight, out):
        g = pl.program_id(0)

        @pl.when(g == 0)
        def _():
            out[...] = jnp.zeros_like(out)

        for k, ref in enumerate((a, b, c, d)):

            @pl.when((g >> 2) == k)
            def _(ref=ref):
                out[...] += dot(ref[...], weight[...])

    return call(
        kernel,
        16,
        where,
        [
            (f, (256, 512), lambda g, w, k=k: (0, jnp.clip(g - 4 * k, 0, 3)))
            for k, f in enumerate(features)
        ]
        + [(weight, (512, 512), lambda g, w: (row_of(g, w), 0))],
        [(shape((256, 512), F32), (256, 512), lambda g, w: (0, 0))],
        deps=deps,
        moved=weight.size * 2 + 256 * 8192 * 2,
        flops=2 * 256 * 8192 * 512,
    )[0]


def squares(value):
    value = value.astype(F32)
    value = value * value
    return value[:, :128] + value[:, 128:256] + value[:, 256:384] + value[:, 384:]


def row_block(g):
    return jnp.where(g < 2, 2 * g + 1, 2 * g - 4)


def project(pieces, projector, where, deps):
    def kernel(where, a, b, c, projector, out, out_squares):
        acc = dot(a[...], projector[0:512, :])
        acc += dot(b[...], projector[512:1024, :])
        out[...] = acc + dot(c[...], projector[1024:1536, :])
        out_squares[...] = squares(a[...]) + squares(b[...]) + squares(c[...])

    return call(
        kernel,
        4,
        where,
        [(p, (256, 512), lambda g, w: (g, 0)) for p in pieces]
        + [(projector, (2048, 512), lambda g, w: (0, 0))],
        [
            (shape((1024, 512), F32), (256, 512), lambda g, w: (g, 0)),
            (shape((1024, 128), F32), (256, 128), lambda g, w: (g, 0)),
        ],
        deps=deps,
        moved=10 << 20,
        flops=2 * 1024 * 1536 * 512,
    )


def packed_extra(power):
    high, mid, low = split3(power)
    column = lax.broadcasted_iota(jnp.int32, (power.shape[0], 128), 1)
    zero = jnp.zeros((), F32)
    high, mid, low = high.astype(F32), mid.astype(F32), low.astype(F32)
    extra = jnp.where(column == 0, high, jnp.where(column == 1, mid, jnp.where(column == 2, low, zero)))
    return extra.astype(BF16)


def project_last(piece, projector, acc, acc_squares, where):
    def kernel(where, piece, projector, acc, acc_squares, out_send, out_keep):
        g = pl.program_id(0)
        total = acc[...] + dot(piece[...], projector[...])
        power = jnp.sum(acc_squares[...] + squares(piece[...]), axis=1, keepdims=True)

        @pl.when(g < 2)
        def _():
            out_send[:, :512] = total.astype(BF16)
            out_send[:, 512:] = packed_extra(power)

        @pl.when(g >= 2)
        def _():
            out_keep[:, :512] = total
            out_keep[:, 512:] = jnp.broadcast_to(power, (256, 128))

    return call(
        kernel,
        4,
        where,
        [
            (piece, (256, 512), lambda g, w: (row_block(g), 0)),
            (projector, (512, 512), lambda g, w: (3, 0)),
            (acc, (256, 512), lambda g, w: (row_block(g), 0)),
            (acc_squares, (256, 128), lambda g, w: (row_block(g), 0)),
        ],
        [
            (shape((512, 640), BF16), (256, 640), lambda g, w: (jnp.minimum(g, 1), 0)),
            (shape((512, 640), F32), (256, 640), lambda g, w: (jnp.maximum(g - 2, 0), 0)),
        ],
        moved=6 << 20,
        flops=2 * 1024 * 512 * 512,
    )


def add_pair(keep, recv, k, packed, where):
    def kernel(where, keep, recv, out):
        total = keep[:, :512] + recv[:, :512].astype(F32)
        power = keep[:, 512:513] + jnp.sum(recv[:, 512:].astype(F32), axis=1, keepdims=True)
        out[:, :512] = total.astype(out.dtype)
        if packed:
            out[:, 512:] = packed_extra(power)
        else:
            out[:, 512:] = jnp.broadcast_to(power, (256, 128))

    return call(
        kernel,
        1,
        where,
        [(v, (256, 640), lambda g, w: (k, 0)) for v in (keep, recv)],
        [(shape((256, 640), BF16 if packed else F32), (256, 640), lambda g, w: (0, 0))],
        moved=2 << 20,
    )[0]


def on_device(
    teacher_input,
    teacher_proj,
    teacher_gain,
    projector,
    student_input,
    student_gain,
    student_weight,
    loss_mask,
):
    core = lax.axis_index("core")
    z, y = lax.axis_index("z"), lax.axis_index("y")
    chip = lax.axis_index(X)

    def address(j):
        total = 0
        for step in range(4):
            d = first_of(j, core, step) & 3
            g = jnp.where(d & 1 == 0, z, y)
            bit = jnp.where(d & 2 == 0, (g ^ (g >> 1)) & 1, g >> 1)
            total = total | (bit << (3 - step))
        return total

    where = jnp.stack([z, y, core, chip, address(0), address(1)]).astype(jnp.int32)

    high, mid, low = split3(student_gain)
    packed = jnp.concatenate(
        [student_input, jnp.stack([high, mid, low]), jnp.zeros((13, 512), BF16)], axis=0
    )
    rows = []
    for j in range(2):
        mine = packed[:, j * 256 : (j + 1) * 256]
        for step in (3, 2, 1, 0):
            mine = jnp.concatenate([mine, swap_zy(mine, j, step)], axis=1)
        rows.append(mine)

    own = [teacher_input] + [swap_x(teacher_input, h) for h in HOPS[1:]]
    own = [[a, swap_core(a)] for a in own]
    streams = [jnp.concatenate(own[2 * j] + own[2 * j + 1], axis=0) for j in range(2)]

    proj = order_columns(teacher_proj, where)

    sent, kept = [], []
    for j in range(2):

        def part(begin, j=j):
            return dot(streams[j], proj[j][:, begin : begin + 512]).astype(BF16)

        sent.append((part(1536), part(1024)))
        kept.append((part(512), part(0)))
    scaled = order_projector(projector, teacher_gain, where, (kept[1][1],))
    ordered = order_rows(student_weight, where, (scaled[0],))

    power_s = sum(jnp.sum(jnp.square(v[:256].astype(F32)), axis=1) for v in rows)
    inv_scale = lax.rsqrt(power_s / DS + EPSILON)
    features = norm_rows(rows[0], rows[1], inv_scale, where, (kept[0][1], kept[1][1]))

    hidden = []
    for j in range(2):
        first, second = swap_zy(sent[j][0], j, 0), swap_zy(sent[j][1], j, 0)
        send = (kept[j][0].astype(F32) + first.astype(F32)).astype(BF16)
        keep = (kept[j][1].astype(F32) + second.astype(F32)).astype(BF16)
        if j == 0:
            (send,) = after([send], features[0])
        recv = swap_zy(send, j, 1)
        for step in (2, 3):
            width = 1024 >> step
            send = (keep[:, width:].astype(F32) + recv[:, width:].astype(F32)).astype(BF16)
            keep = (keep[:, :width].astype(F32) + recv[:, :width].astype(F32)).astype(BF16)
            recv = swap_zy(send, j, step)
        hidden.append((keep.astype(F32) + recv.astype(F32)).astype(BF16))

    pieces = []
    for j in range(2):
        mine = hidden[j]
        for step in (3, 2):
            mine = jnp.concatenate([mine, swap_zy(mine, j, step)], axis=1)
        other = swap_zy(mine, j, 1)
        pieces.append([mine, other, swap_zy(mine, j, 0), swap_zy(other, j, 0)])

    crossed = [swap_x(f, h) for f, h in zip(features[1:], HOPS[1:])]
    of_chips = [features[0]] + crossed
    features_own = jnp.concatenate(
        [lax.dynamic_slice_in_dim(v, core * 1024, 1024, 1) for v in of_chips], axis=0
    )
    features_send = jnp.concatenate(
        [lax.dynamic_slice_in_dim(v, (1 - core) * 1024, 1024, 1) for v in of_chips], axis=0
    )
    product = forward(features, student_weight, where, (pieces[0][0], pieces[1][0], ordered[0]))

    sums, sends = [], []
    for j in range(2):
        deps = (product, features_own, features_send) if j == 0 else ()
        acc, acc_squares = project(pieces[j][:3], scaled[j], where, deps)
        send, keep = project_last(pieces[j][3], scaled[j], acc, acc_squares, where)
        sends.append(send)
        recv = swap_core(send)
        for k in range(2):
            hop = HOPS[2 * j + k]
            part = add_pair(keep, recv, k, bool(hop), where)
            sums.append(swap_x(part, hop) if hop else part)
    features_next = swap_core(after([features_send], *sends)[0])
    target = sum(s[:, :512].astype(F32) for s in sums)
    power = sums[0][:, 512] + sum(jnp.sum(s[:, 512:].astype(F32), axis=1) for s in sums[1:])
    target = target * lax.rsqrt(power / DT + EPSILON)[:, None]
    target = target.astype(BF16).astype(F32)

    inputs = student_input.astype(F32)
    error = loss_mask.astype(F32)[:, None] * (inputs + product - target)
    error_b = error.astype(BF16)

    inner = jnp.sum(error_b.astype(F32) * product, axis=1) / inv_scale
    slope = inv_scale**3 * inner / DS
    back, started = [], []
    for j in range(2):
        gain = jnp.sum(rows[j][256:259].astype(F32), axis=0)

        def piece(begin, j=j, gain=gain):
            end = begin + 1024
            value = dot_t(error_b, ordered[j][begin:end])
            value = value * inv_scale[:, None] * gain[begin:end]
            return (value - rows[j][:256, begin:end].astype(F32) * slope[:, None]).astype(BF16)

        first, second = piece(3072), piece(2048)
        started += [first, second]
        first, second = swap_zy(first, j, 0), swap_zy(second, j, 0)
        send = (piece(1024).astype(F32) + first.astype(F32)).astype(BF16)
        keep = (piece(0).astype(F32) + second.astype(F32)).astype(BF16)
        recv = swap_zy(send, j, 1)
        for step in (2, 3):
            width = 2048 >> step
            send = (keep[:, width:].astype(F32) + recv[:, width:].astype(F32)).astype(BF16)
            keep = (keep[:, :width].astype(F32) + recv[:, :width].astype(F32)).astype(BF16)
            recv = swap_zy(send, j, step)
        back.append(keep.astype(F32) + recv.astype(F32))
    input_grad = error + jnp.concatenate(back, axis=1)

    (errors,) = after([error_b], *started)
    errors_own = jnp.concatenate([errors] + [swap_x(errors, h) for h in HOPS[1:]], axis=0)
    errors_next = swap_core(errors_own)
    contract = (((0,), (0,)), ((), ()))
    weight_grad = lax.dot_general(
        features_own, errors_own, contract, preferred_element_type=F32
    ) + lax.dot_general(features_next, errors_next, contract, preferred_element_type=F32)
    return (weight_grad, input_grad.astype(BF16))


def solution(mesh):
    fine = Mesh(mesh.devices.reshape(2, 4, 4, 2, 2), ("section", "z", "y", "xhi", "core"))
    d, t = ("section", "xhi", "core"), ("z", "y")
    in_specs = (P(d, t), P(t, d), P(d), P(d, t), P(d, t), P(t), P(None, t), P(d))
    out_specs = (P(d, t), P(d, t))
    return jax.shard_map(
        on_device, mesh=fine, in_specs=in_specs, out_specs=out_specs, check_vma=False
    )
```

```python
import jax
import jax.numpy as jnp
from jax import lax
from jax.experimental import pallas as pl
from jax.experimental.pallas import tpu as pltpu
from jax.sharding import Mesh, PartitionSpec as P

DT = 16384
DS = 8192
EPSILON = 1e-05
F32 = jnp.float32
BF16 = jnp.bfloat16

X = ("section", "xhi")
ZYC = ("z", "y", "core")
HOPS = (0, 2, 3, 1)
FLIP = ((1, 0), (0, 1), (3, 0), (0, 3))
ANYWHERE = pl.BlockSpec(memory_space=pl.ANY)


def dot(a, b):
    return jnp.dot(a, b, preferred_element_type=F32)


def dot_t(a, b):
    return lax.dot_general(a, b, (((1,), (1,)), ((), ())), preferred_element_type=F32)


def first_of(j, core, step):
    return (3 - core if j else core) + step


def swap_zy(value, j, step):
    perm = []
    for z in range(4):
        for y in range(4):
            for core in range(2):
                dz, dy = FLIP[first_of(j, core, step) % 4]
                perm.append(((z * 4 + y) * 2 + core, ((z ^ dz) * 4 + (y ^ dy)) * 2 + core))
    return lax.ppermute(value, ZYC, perm)


def swap_x(value, r):
    return lax.ppermute(value, X, [(j, j ^ r) for j in range(4)])


def swap_core(value):
    return lax.ppermute(value, "core", [(0, 1), (1, 0)])


def split3(value):
    high = value.astype(BF16)
    rest = value - high.astype(F32)
    mid = rest.astype(BF16)
    low = (rest - mid.astype(F32)).astype(BF16)
    return high, mid, low


def call(kernel, grid, scalars, ins, outs, deps=(), scratch=(), moved=0, flops=0):
    n, m = len(ins), len(outs)

    def body(where, *refs):
        kernel(where, *refs[:n], *refs[n + len(deps) :])

    result = pl.pallas_call(
        body,
        grid_spec=pltpu.PrefetchScalarGridSpec(
            num_scalar_prefetch=1,
            grid=(grid,),
            in_specs=[pl.BlockSpec(b, i) for _, b, i in ins] + [ANYWHERE] * len(deps),
            out_specs=[pl.BlockSpec(b, i) for _, b, i in outs],
            scratch_shapes=list(scratch),
        ),
        out_shape=[s for s, _, _ in outs],
        compiler_params=pltpu.CompilerParams(vmem_limit_bytes=16 << 20),
        cost_estimate=pl.CostEstimate(flops=flops, bytes_accessed=moved, transcendentals=0),
    )(scalars, *[a for a, _, _ in ins], *deps)
    return result


def shape(dims, dtype):
    return jax.ShapeDtypeStruct(dims, dtype)


def nothing(*refs):
    pass


def after(values, *deps):
    n = len(values)
    return pl.pallas_call(
        nothing,
        in_specs=[ANYWHERE] * (n + len(deps)),
        out_specs=[ANYWHERE] * n,
        out_shape=[shape(v.shape, v.dtype) for v in values],
        input_output_aliases={i: i for i in range(n)},
        cost_estimate=pl.CostEstimate(flops=0, bytes_accessed=0, transcendentals=0),
    )(*values, *deps)


def block_of(t, where, j):
    gz, gy = (t >> 2) ^ where[0], (t & 3) ^ where[1]
    r = 0
    for step in range(4):
        d = first_of(j, where[2], step) & 3
        g = jnp.where(d & 1 == 0, gz, gy)
        gray = jnp.where(d & 2 == 0, (g ^ (g >> 1)) & 1, g >> 1)
        r = r | (gray << (3 - step))
    return r


def order_columns(proj, where):
    def kernel(where, a, b, out_a, out_b):
        out_a[...] = a[...]
        out_b[...] = b[...]

    return call(
        kernel,
        16,
        where,
        [(proj, (1024, 128), lambda r, w, j=j: (0, r ^ w[4 + j])) for j in range(2)],
        [(shape((1024, 2048), BF16), (1024, 128), lambda r, w: (0, r)) for j in range(2)],
        moved=4 * proj.size * 2,
    )


def order_projector(projector, gain, where, deps):
    def kernel(where, a, b, gain_a, gain_b, out_a, out_b):
        out_a[...] = (a[...].astype(F32) * gain_a[...]).astype(BF16)
        out_b[...] = (b[...].astype(F32) * gain_b[...]).astype(BF16)

    gain = gain[:, None]
    return call(
        kernel,
        16,
        where,
        [(projector, (128, 512), lambda r, w, j=j: (r ^ w[4 + j], 0)) for j in range(2)]
        + [(gain, (128, 1), lambda r, w, j=j: (r ^ w[4 + j], 0)) for j in range(2)],
        [(shape((2048, 512), BF16), (128, 512), lambda r, w: (r, 0)) for j in range(2)],
        deps=deps,
        moved=4 * projector.size * 2,
    )


def tensor_of(g, where):
    k = g >> 1
    hop = jnp.where(k < 2, 0, jnp.where(k < 4, 4, jnp.where(k < 6, 6, 2)))
    return (((where[3] * 2 + where[2]) ^ (hop | (k & 1))) << 1) | (g & 1)


def visit(*begins):
    def block(g):
        total = jnp.clip(g - begins[0], 0, 1)
        for begin in begins[1:]:
            total += jnp.clip(g - begin + 1, 0, 2)
        return total

    return block


PARTS = [(1024, visit(4 * h)) for h in range(4)] + [(2048, visit(6, 10)), (2048, visit(2, 14))]
PLACE = (0, 5, 1, 4, 2, 4, 3, 5)


def norm_rows(rows, inv_scale, where, deps):
    def kernel(where, scale, *refs):
        g = pl.program_id(0)
        outs = refs[2:]
        for k in range(8):

            @pl.when((g >> 1) == k)
            def _(k=k):
                out = outs[PLACE[k]]
                for j in range(2):
                    value = refs[j][...].astype(F32)
                    gain = value[256:257] + value[257:258] + value[258:259]
                    out[:, j * 256 : (j + 1) * 256] = (
                        value[:256] * scale[...] * gain
                    ).astype(BF16)

    return call(
        kernel,
        16,
        where,
        [(inv_scale[:, None], (256, 1), lambda g, w: (0, 0))]
        + [
            (rows[j], (272, 256), lambda g, w, j=j: (0, block_of(tensor_of(g, w), w, j)))
            for j in range(2)
        ],
        [
            (shape((256, width), BF16), (256, 512), lambda g, w, f=f: (0, f(g)))
            for width, f in PARTS
        ],
        deps=deps,
        moved=4 * 272 * 4096 * 2,
    )


def forward(features, weight, where, deps):
    def kernel(where, *refs):
        weight, out, out_a, out_b = refs[6:]
        g = pl.program_id(0)

        @pl.when(g == 0)
        def _():
            out[...] = jnp.zeros_like(out)

        for k in range(8):

            @pl.when((g >> 1) == k)
            def _(k=k):
                out[...] += dot(refs[PLACE[k]][...], weight[...])

        out_a[...] = weight[:256, :]
        out_b[...] = weight[256:, :]

    return call(
        kernel,
        16,
        where,
        [
            (v, (256, 512), lambda g, w, f=f: (0, f(g)))
            for v, (_, f) in zip(features, PARTS)
        ]
        + [(weight, (512, 512), lambda g, w: (tensor_of(g, w), 0))],
        [(shape((256, 512), F32), (256, 512), lambda g, w: (0, 0))]
        + [
            (
                shape((4096, 512), BF16),
                (256, 512),
                lambda g, w, j=j: (block_of(tensor_of(g, w), w, j), 0),
            )
            for j in range(2)
        ],
        deps=deps,
        moved=2 * weight.size * 2 + 256 * 8192 * 2,
        flops=2 * 256 * 8192 * 512,
    )


def squares(value):
    value = value.astype(F32)
    value = value * value
    return value[:, :128] + value[:, 128:256] + value[:, 256:384] + value[:, 384:]


def row_block(g):
    return jnp.where(g < 2, 2 * g + 1, 2 * g - 4)


def project(pieces, projector, where, deps):
    def kernel(where, a, b, c, projector, out, out_squares):
        acc = dot(a[...], projector[0:512, :])
        acc += dot(b[...], projector[512:1024, :])
        out[...] = acc + dot(c[...], projector[1024:1536, :])
        out_squares[...] = squares(a[...]) + squares(b[...]) + squares(c[...])

    return call(
        kernel,
        4,
        where,
        [(p, (256, 512), lambda g, w: (g, 0)) for p in pieces]
        + [(projector, (2048, 512), lambda g, w: (0, 0))],
        [
            (shape((1024, 512), F32), (256, 512), lambda g, w: (g, 0)),
            (shape((1024, 128), F32), (256, 128), lambda g, w: (g, 0)),
        ],
        deps=deps,
        moved=10 << 20,
        flops=2 * 1024 * 1536 * 512,
    )


def packed_extra(power):
    high, mid, low = split3(power)
    column = lax.broadcasted_iota(jnp.int32, (power.shape[0], 128), 1)
    zero = jnp.zeros((), F32)
    high, mid, low = high.astype(F32), mid.astype(F32), low.astype(F32)
    extra = jnp.where(column == 0, high, jnp.where(column == 1, mid, jnp.where(column == 2, low, zero)))
    return extra.astype(BF16)


def project_last(piece, projector, acc, acc_squares, where):
    def kernel(where, piece, projector, acc, acc_squares, out_send, out_keep):
        g = pl.program_id(0)
        total = acc[...] + dot(piece[...], projector[...])
        power = jnp.sum(acc_squares[...] + squares(piece[...]), axis=1, keepdims=True)

        @pl.when(g < 2)
        def _():
            out_send[:, :512] = total.astype(BF16)
            out_send[:, 512:] = packed_extra(power)

        @pl.when(g >= 2)
        def _():
            out_keep[:, :512] = total
            out_keep[:, 512:] = jnp.broadcast_to(power, (256, 128))

    return call(
        kernel,
        4,
        where,
        [
            (piece, (256, 512), lambda g, w: (row_block(g), 0)),
            (projector, (512, 512), lambda g, w: (3, 0)),
            (acc, (256, 512), lambda g, w: (row_block(g), 0)),
            (acc_squares, (256, 128), lambda g, w: (row_block(g), 0)),
        ],
        [
            (shape((512, 640), BF16), (256, 640), lambda g, w: (jnp.minimum(g, 1), 0)),
            (shape((512, 640), F32), (256, 640), lambda g, w: (jnp.maximum(g - 2, 0), 0)),
        ],
        moved=6 << 20,
        flops=2 * 1024 * 512 * 512,
    )


def add_pair(keep, recv, k, packed, where):
    def kernel(where, keep, recv, out):
        total = keep[:, :512] + recv[:, :512].astype(F32)
        power = keep[:, 512:513] + jnp.sum(recv[:, 512:].astype(F32), axis=1, keepdims=True)
        out[:, :512] = total.astype(out.dtype)
        if packed:
            out[:, 512:] = packed_extra(power)
        else:
            out[:, 512:] = jnp.broadcast_to(power, (256, 128))

    return call(
        kernel,
        1,
        where,
        [(v, (256, 640), lambda g, w: (k, 0)) for v in (keep, recv)],
        [(shape((256, 640), BF16 if packed else F32), (256, 640), lambda g, w: (0, 0))],
        moved=2 << 20,
    )[0]


def on_device(
    teacher_input,
    teacher_proj,
    teacher_gain,
    projector,
    student_input,
    student_gain,
    student_weight,
    loss_mask,
):
    core = lax.axis_index("core")
    z, y = lax.axis_index("z"), lax.axis_index("y")
    chip = lax.axis_index(X)

    def address(j):
        total = 0
        for step in range(4):
            d = first_of(j, core, step) & 3
            g = jnp.where(d & 1 == 0, z, y)
            bit = jnp.where(d & 2 == 0, (g ^ (g >> 1)) & 1, g >> 1)
            total = total | (bit << (3 - step))
        return total

    where = jnp.stack([z, y, core, chip, address(0), address(1)]).astype(jnp.int32)

    high, mid, low = split3(student_gain)
    packed = jnp.concatenate(
        [student_input, jnp.stack([high, mid, low]), jnp.zeros((13, 512), BF16)], axis=0
    )
    rows = []
    for j in range(2):
        mine = packed[:, j * 256 : (j + 1) * 256]
        for step in (3, 2, 1, 0):
            mine = jnp.concatenate([mine, swap_zy(mine, j, step)], axis=1)
        rows.append(mine)

    own = [teacher_input] + [swap_x(teacher_input, h) for h in HOPS[1:]]
    own = [[a, swap_core(a)] for a in own]
    streams = [jnp.concatenate(own[2 * j] + own[2 * j + 1], axis=0) for j in range(2)]

    proj = order_columns(teacher_proj, where)

    sent, kept = [], []
    for j in range(2):

        def part(begin, j=j):
            return dot(streams[j], proj[j][:, begin : begin + 512]).astype(BF16)

        sent.append((part(1536), part(1024)))
        kept.append((part(512), part(0)))
    scaled = order_projector(projector, teacher_gain, where, (kept[1][1],))

    power_s = sum(jnp.sum(jnp.square(v[:256].astype(F32)), axis=1) for v in rows)
    inv_scale = lax.rsqrt(power_s / DS + EPSILON)
    features = norm_rows(rows, inv_scale, where, (kept[0][1], kept[1][1]))

    hidden = []
    for j in range(2):
        first, second = swap_zy(sent[j][0], j, 0), swap_zy(sent[j][1], j, 0)
        send = (kept[j][0].astype(F32) + first.astype(F32)).astype(BF16)
        keep = (kept[j][1].astype(F32) + second.astype(F32)).astype(BF16)
        if j == 0:
            (send,) = after([send], features[0])
        recv = swap_zy(send, j, 1)
        for step in (2, 3):
            width = 1024 >> step
            send = (keep[:, width:].astype(F32) + recv[:, width:].astype(F32)).astype(BF16)
            keep = (keep[:, :width].astype(F32) + recv[:, :width].astype(F32)).astype(BF16)
            recv = swap_zy(send, j, step)
        hidden.append((keep.astype(F32) + recv.astype(F32)).astype(BF16))

    pieces = []
    for j in range(2):
        mine = hidden[j]
        for step in (3, 2):
            mine = jnp.concatenate([mine, swap_zy(mine, j, step)], axis=1)
        other = swap_zy(mine, j, 1)
        pieces.append([mine, other, swap_zy(mine, j, 0), swap_zy(other, j, 0)])

    sums, parts = [], []
    for j in range(2):
        acc, acc_squares = project(pieces[j][:3], scaled[j], where, ())
        send, keep = project_last(pieces[j][3], scaled[j], acc, acc_squares, where)
        recv = swap_core(send)
        for k in range(2):
            hop = HOPS[2 * j + k]
            part = add_pair(keep, recv, k, bool(hop), where)
            parts.append(part)
            sums.append(swap_x(part, hop) if hop else part)
    product, *ordered = forward(features, student_weight, where, parts)
    target = sum(s[:, :512].astype(F32) for s in sums)
    power = sums[0][:, 512] + sum(jnp.sum(s[:, 512:].astype(F32), axis=1) for s in sums[1:])
    target = target * lax.rsqrt(power / DT + EPSILON)[:, None]
    target = target.astype(BF16).astype(F32)

    inputs = student_input.astype(F32)
    error = loss_mask.astype(F32)[:, None] * (inputs + product - target)
    error_b = error.astype(BF16)

    inner = jnp.sum(error_b.astype(F32) * product, axis=1) / inv_scale
    slope = inv_scale**3 * inner / DS
    gains = [jnp.sum(v[256:259].astype(F32), axis=0) for v in rows]

    def outer(k):
        return lax.dot_general(
            features[k], error_b, (((0,), (0,)), ((), ())), preferred_element_type=F32
        )

    near, far = [swap_core(outer(k).astype(BF16)).astype(F32) for k in (4, 5)]
    shares = [
        outer(0) + far[:1024],
        outer(1) + near[:1024],
        outer(2) + near[1024:],
        outer(3) + far[1024:],
    ]

    sides = ((slice(0, 256), 1, 2), (slice(256, 512), 2, 1))
    carried = [
        jnp.concatenate([shares[a][:, cut], shares[3][:, cut]], axis=0).astype(BF16)
        for cut, a, _ in sides
    ]
    landed = [swap_x(v, HOPS[a]) for v, (_, a, _) in zip(carried, sides)]

    def piece(j, begin):
        end = begin + 1024
        value = dot_t(error_b, ordered[j][begin:end])
        value = value * inv_scale[:, None] * gains[j][begin:end]
        return (value - rows[j][:256, begin:end].astype(F32) * slope[:, None]).astype(BF16)

    def total(a, b):
        return (a.astype(F32) + b.astype(F32)).astype(BF16)

    first = [piece(0, 3072), piece(1, 3072)]
    second = after([piece(0, 2048), piece(1, 2048)], *carried)
    high = [piece(0, 1024), piece(1, 1024)]
    low = [piece(0, 0), piece(1, 0)]
    first = [swap_zy(first[j], j, 0) for j in range(2)]
    second = [swap_zy(second[j], j, 0) for j in range(2)]
    send = [total(high[j], first[j]) for j in range(2)]
    recv = [swap_zy(send[j], j, 1) for j in range(2)]
    keep = [total(low[j], second[j]) for j in range(2)]
    for step in (2, 3):
        width = 2048 >> step
        send = [total(keep[j][:, width:], recv[j][:, width:]) for j in range(2)]
        if step == 3:
            send[0] = after([send[0]], *landed)[0]
        keep = [total(keep[j][:, :width], recv[j][:, :width]) for j in range(2)]
        recv = [swap_zy(send[j], j, step) for j in range(2)]
    back = [keep[j].astype(F32) + recv[j].astype(F32) for j in range(2)]
    input_grad = error + jnp.concatenate(back, axis=1)

    ends = []
    for value, (cut, a, b) in zip(landed, sides):
        value = value.astype(F32)
        last = swap_x((shares[b][:, cut] + value[1024:]).astype(BF16), HOPS[b])
        ends.append(shares[0][:, cut] + value[:1024] + last.astype(F32))
    weight_grad = jnp.concatenate(ends, axis=1)
    return (weight_grad, input_grad.astype(BF16))


def solution(mesh):
    fine = Mesh(mesh.devices.reshape(2, 4, 4, 2, 2), ("section", "z", "y", "xhi", "core"))
    d, t = ("section", "xhi", "core"), ("z", "y")
    in_specs = (P(d, t), P(t, d), P(d), P(d, t), P(d, t), P(t), P(None, t), P(d))
    out_specs = (P(d, t), P(d, t))
    return jax.shard_map(
        on_device, mesh=fine, in_specs=in_specs, out_specs=out_specs, check_vma=False
    )
```

```python
import jax
import jax.numpy as jnp
from jax import lax
from jax.experimental import pallas as pl
from jax.experimental.pallas import tpu as pltpu
from jax.sharding import Mesh, PartitionSpec as P

DT = 16384
DS = 8192
EPSILON = 1e-05
F32 = jnp.float32
BF16 = jnp.bfloat16

X = ("section", "xhi")
ZYC = ("z", "y", "core")
HOPS = (0, 2, 3, 1)
FLIP = ((1, 0), (0, 1), (3, 0), (0, 3))
ANYWHERE = pl.BlockSpec(memory_space=pl.ANY)


def dot(a, b):
    return jnp.dot(a, b, preferred_element_type=F32)


def dot_t(a, b):
    return lax.dot_general(a, b, (((1,), (1,)), ((), ())), preferred_element_type=F32)


def first_of(j, core, step):
    return (3 - core if j else core) + step


def swap_zy(value, j, step):
    perm = []
    for z in range(4):
        for y in range(4):
            for core in range(2):
                dz, dy = FLIP[first_of(j, core, step) % 4]
                perm.append(((z * 4 + y) * 2 + core, ((z ^ dz) * 4 + (y ^ dy)) * 2 + core))
    return lax.ppermute(value, ZYC, perm)


def swap_x(value, r):
    return lax.ppermute(value, X, [(j, j ^ r) for j in range(4)])


def swap_core(value):
    return lax.ppermute(value, "core", [(0, 1), (1, 0)])


def split3(value):
    high = value.astype(BF16)
    rest = value - high.astype(F32)
    mid = rest.astype(BF16)
    low = (rest - mid.astype(F32)).astype(BF16)
    return high, mid, low


def call(kernel, grid, scalars, ins, outs, deps=(), scratch=(), moved=0, flops=0):
    n, m = len(ins), len(outs)

    def body(where, *refs):
        kernel(where, *refs[:n], *refs[n + len(deps) :])

    result = pl.pallas_call(
        body,
        grid_spec=pltpu.PrefetchScalarGridSpec(
            num_scalar_prefetch=1,
            grid=(grid,),
            in_specs=[pl.BlockSpec(b, i) for _, b, i in ins] + [ANYWHERE] * len(deps),
            out_specs=[pl.BlockSpec(b, i) for _, b, i in outs],
            scratch_shapes=list(scratch),
        ),
        out_shape=[s for s, _, _ in outs],
        compiler_params=pltpu.CompilerParams(vmem_limit_bytes=16 << 20),
        cost_estimate=pl.CostEstimate(flops=flops, bytes_accessed=moved, transcendentals=0),
    )(scalars, *[a for a, _, _ in ins], *deps)
    return result


def shape(dims, dtype):
    return jax.ShapeDtypeStruct(dims, dtype)


def nothing(*refs):
    pass


def after(values, *deps):
    n = len(values)
    return pl.pallas_call(
        nothing,
        in_specs=[ANYWHERE] * (n + len(deps)),
        out_specs=[ANYWHERE] * n,
        out_shape=[shape(v.shape, v.dtype) for v in values],
        input_output_aliases={i: i for i in range(n)},
        cost_estimate=pl.CostEstimate(flops=0, bytes_accessed=0, transcendentals=0),
    )(*values, *deps)


def block_of(t, where, j):
    gz, gy = (t >> 2) ^ where[0], (t & 3) ^ where[1]
    r = 0
    for step in range(4):
        d = first_of(j, where[2], step) & 3
        g = jnp.where(d & 1 == 0, gz, gy)
        gray = jnp.where(d & 2 == 0, (g ^ (g >> 1)) & 1, g >> 1)
        r = r | (gray << (3 - step))
    return r


def order_columns(proj, where):
    def kernel(where, a, b, out_a, out_b):
        out_a[...] = a[...]
        out_b[...] = b[...]

    return call(
        kernel,
        16,
        where,
        [(proj, (1024, 128), lambda r, w, j=j: (0, r ^ w[4 + j])) for j in range(2)],
        [(shape((1024, 2048), BF16), (1024, 128), lambda r, w: (0, r)) for j in range(2)],
        moved=4 * proj.size * 2,
    )


def order_projector(projector, gain, where, deps):
    def kernel(where, a, b, gain_a, gain_b, out_a, out_b):
        out_a[...] = (a[...].astype(F32) * gain_a[...]).astype(BF16)
        out_b[...] = (b[...].astype(F32) * gain_b[...]).astype(BF16)

    gain = gain[:, None]
    return call(
        kernel,
        16,
        where,
        [(projector, (128, 512), lambda r, w, j=j: (r ^ w[4 + j], 0)) for j in range(2)]
        + [(gain, (128, 1), lambda r, w, j=j: (r ^ w[4 + j], 0)) for j in range(2)],
        [(shape((2048, 512), BF16), (128, 512), lambda r, w: (r, 0)) for j in range(2)],
        deps=deps,
        moved=4 * projector.size * 2,
    )


def tensor_of(g, where):
    k = g >> 1
    hop = jnp.where(k < 2, 0, jnp.where(k < 4, 4, jnp.where(k < 6, 6, 2)))
    return (((where[3] * 2 + where[2]) ^ (hop | (k & 1))) << 1) | (g & 1)


def visit(*begins):
    def block(g):
        total = jnp.clip(g - begins[0], 0, 1)
        for begin in begins[1:]:
            total += jnp.clip(g - begin + 1, 0, 2)
        return total

    return block


PARTS = [(1024, visit(4 * h)) for h in range(4)] + [(2048, visit(6, 10)), (2048, visit(2, 14))]
PLACE = (0, 5, 1, 4, 2, 4, 3, 5)


def norm_rows(rows, inv_scale, where, deps):
    def kernel(where, scale, *refs):
        g = pl.program_id(0)
        outs = refs[2:]
        for k in range(8):

            @pl.when((g >> 1) == k)
            def _(k=k):
                out = outs[PLACE[k]]
                for j in range(2):
                    value = refs[j][...].astype(F32)
                    gain = value[256:257] + value[257:258] + value[258:259]
                    out[:, j * 256 : (j + 1) * 256] = (
                        value[:256] * scale[...] * gain
                    ).astype(BF16)

    return call(
        kernel,
        16,
        where,
        [(inv_scale[:, None], (256, 1), lambda g, w: (0, 0))]
        + [
            (rows[j], (272, 256), lambda g, w, j=j: (0, block_of(tensor_of(g, w), w, j)))
            for j in range(2)
        ],
        [
            (shape((256, width), BF16), (256, 512), lambda g, w, f=f: (0, f(g)))
            for width, f in PARTS
        ],
        deps=deps,
        moved=4 * 272 * 4096 * 2,
    )


def forward(features, weight, where, deps):
    def kernel(where, *refs):
        weight, out, out_a, out_b = refs[6:]
        g = pl.program_id(0)

        @pl.when(g == 0)
        def _():
            out[...] = jnp.zeros_like(out)

        for k in range(8):

            @pl.when((g >> 1) == k)
            def _(k=k):
                out[...] += dot(refs[PLACE[k]][...], weight[...])

        out_a[...] = weight[:256, :]
        out_b[...] = weight[256:, :]

    return call(
        kernel,
        16,
        where,
        [
            (v, (256, 512), lambda g, w, f=f: (0, f(g)))
            for v, (_, f) in zip(features, PARTS)
        ]
        + [(weight, (512, 512), lambda g, w: (tensor_of(g, w), 0))],
        [(shape((256, 512), F32), (256, 512), lambda g, w: (0, 0))]
        + [
            (
                shape((4096, 512), BF16),
                (256, 512),
                lambda g, w, j=j: (block_of(tensor_of(g, w), w, j), 0),
            )
            for j in range(2)
        ],
        deps=deps,
        moved=2 * weight.size * 2 + 256 * 8192 * 2,
        flops=2 * 256 * 8192 * 512,
    )


def squares(value):
    value = value.astype(F32)
    value = value * value
    return value[:, :128] + value[:, 128:256] + value[:, 256:384] + value[:, 384:]


def row_block(g):
    return jnp.where(g < 2, 2 * g + 1, 2 * g - 4)


def project(pieces, projector, where, deps):
    def kernel(where, a, b, c, projector, out, out_squares):
        acc = dot(a[...], projector[0:512, :])
        acc += dot(b[...], projector[512:1024, :])
        out[...] = acc + dot(c[...], projector[1024:1536, :])
        out_squares[...] = squares(a[...]) + squares(b[...]) + squares(c[...])

    return call(
        kernel,
        4,
        where,
        [(p, (256, 512), lambda g, w: (g, 0)) for p in pieces]
        + [(projector, (2048, 512), lambda g, w: (0, 0))],
        [
            (shape((1024, 512), F32), (256, 512), lambda g, w: (g, 0)),
            (shape((1024, 128), F32), (256, 128), lambda g, w: (g, 0)),
        ],
        deps=deps,
        moved=10 << 20,
        flops=2 * 1024 * 1536 * 512,
    )


def packed_extra(power):
    high, mid, low = split3(power)
    column = lax.broadcasted_iota(jnp.int32, (power.shape[0], 128), 1)
    zero = jnp.zeros((), F32)
    high, mid, low = high.astype(F32), mid.astype(F32), low.astype(F32)
    extra = jnp.where(column == 0, high, jnp.where(column == 1, mid, jnp.where(column == 2, low, zero)))
    return extra.astype(BF16)


def project_last(piece, projector, acc, acc_squares, where, deps):
    def kernel(where, piece, projector, acc, acc_squares, out_send, out_keep):
        g = pl.program_id(0)
        total = acc[...] + dot(piece[...], projector[...])
        power = jnp.sum(acc_squares[...] + squares(piece[...]), axis=1, keepdims=True)

        @pl.when(g < 2)
        def _():
            out_send[:, :512] = total.astype(BF16)
            out_send[:, 512:] = packed_extra(power)

        @pl.when(g >= 2)
        def _():
            out_keep[:, :512] = total
            out_keep[:, 512:] = jnp.broadcast_to(power, (256, 128))

    return call(
        kernel,
        4,
        where,
        [
            (piece, (256, 512), lambda g, w: (row_block(g), 0)),
            (projector, (512, 512), lambda g, w: (3, 0)),
            (acc, (256, 512), lambda g, w: (row_block(g), 0)),
            (acc_squares, (256, 128), lambda g, w: (row_block(g), 0)),
        ],
        [
            (shape((512, 640), BF16), (256, 640), lambda g, w: (jnp.minimum(g, 1), 0)),
            (shape((512, 640), F32), (256, 640), lambda g, w: (jnp.maximum(g - 2, 0), 0)),
        ],
        deps=deps,
        moved=6 << 20,
        flops=2 * 1024 * 512 * 512,
    )


def add_pair(keep, recv, k, packed, where):
    def kernel(where, keep, recv, out):
        total = keep[:, :512] + recv[:, :512].astype(F32)
        power = keep[:, 512:513] + jnp.sum(recv[:, 512:].astype(F32), axis=1, keepdims=True)
        out[:, :512] = total.astype(out.dtype)
        if packed:
            out[:, 512:] = packed_extra(power)
        else:
            out[:, 512:] = jnp.broadcast_to(power, (256, 128))

    return call(
        kernel,
        1,
        where,
        [(v, (256, 640), lambda g, w: (k, 0)) for v in (keep, recv)],
        [(shape((256, 640), BF16 if packed else F32), (256, 640), lambda g, w: (0, 0))],
        moved=2 << 20,
    )[0]


def on_device(
    teacher_input,
    teacher_proj,
    teacher_gain,
    projector,
    student_input,
    student_gain,
    student_weight,
    loss_mask,
):
    core = lax.axis_index("core")
    z, y = lax.axis_index("z"), lax.axis_index("y")
    chip = lax.axis_index(X)

    def address(j):
        total = 0
        for step in range(4):
            d = first_of(j, core, step) & 3
            g = jnp.where(d & 1 == 0, z, y)
            bit = jnp.where(d & 2 == 0, (g ^ (g >> 1)) & 1, g >> 1)
            total = total | (bit << (3 - step))
        return total

    where = jnp.stack([z, y, core, chip, address(0), address(1)]).astype(jnp.int32)

    high, mid, low = split3(student_gain)
    packed = jnp.concatenate(
        [student_input, jnp.stack([high, mid, low]), jnp.zeros((13, 512), BF16)], axis=0
    )
    rows = []
    for j in range(2):
        mine = packed[:, j * 256 : (j + 1) * 256]
        for step in (3, 2, 1, 0):
            mine = jnp.concatenate([mine, swap_zy(mine, j, step)], axis=1)
        rows.append(mine)

    own = [teacher_input] + [swap_x(teacher_input, h) for h in HOPS[1:]]
    own = [[a, swap_core(a)] for a in own]
    streams = [jnp.concatenate(own[2 * j] + own[2 * j + 1], axis=0) for j in range(2)]

    proj = order_columns(teacher_proj, where)

    sent, kept = [], []
    for j in range(2):

        def part(begin, j=j):
            return dot(streams[j], proj[j][:, begin : begin + 512]).astype(BF16)

        sent.append((part(1536), part(1024)))
        kept.append((part(512), part(0)))
    scaled = order_projector(projector, teacher_gain, where, (kept[1][1],))

    power_s = sum(jnp.sum(jnp.square(v[:256].astype(F32)), axis=1) for v in rows)
    inv_scale = lax.rsqrt(power_s / DS + EPSILON)
    features = norm_rows(rows, inv_scale, where, (kept[0][1], kept[1][1]))

    hidden = []
    for j in range(2):
        first, second = swap_zy(sent[j][0], j, 0), swap_zy(sent[j][1], j, 0)
        send = (kept[j][0].astype(F32) + first.astype(F32)).astype(BF16)
        keep = (kept[j][1].astype(F32) + second.astype(F32)).astype(BF16)
        if j == 0:
            (send,) = after([send], *rows)
        recv = swap_zy(send, j, 1)
        for step in (2, 3):
            width = 1024 >> step
            send = (keep[:, width:].astype(F32) + recv[:, width:].astype(F32)).astype(BF16)
            keep = (keep[:, :width].astype(F32) + recv[:, :width].astype(F32)).astype(BF16)
            recv = swap_zy(send, j, step)
        hidden.append((keep.astype(F32) + recv.astype(F32)).astype(BF16))

    pieces = []
    for j in range(2):
        mine = hidden[j]
        for step in (3, 2):
            mine = jnp.concatenate([mine, swap_zy(mine, j, step)], axis=1)
        other = swap_zy(mine, j, 1)
        pieces.append([mine, other, swap_zy(mine, j, 0), swap_zy(other, j, 0)])

    sums, parts = [], []
    begun = [
        project(pieces[j][:3], scaled[j], where, (features[0],) if j == 0 else ())
        for j in range(2)
    ]
    for j in (1, 0):
        deps = (begun[0][0],) if j else ()
        send, keep = project_last(pieces[j][3], scaled[j], *begun[j], where, deps)
        recv = swap_core(send)
        for k in range(2):
            hop = HOPS[2 * j + k]
            part = add_pair(keep, recv, k, bool(hop), where)
            parts.append(part)
            sums.append(swap_x(part, hop) if hop else part)
    own = sums.pop(2)
    sums = [own] + sums
    product, *ordered = forward(features, student_weight, where, parts)
    target = sum(s[:, :512].astype(F32) for s in sums)
    power = sums[0][:, 512] + sum(jnp.sum(s[:, 512:].astype(F32), axis=1) for s in sums[1:])
    target = target * lax.rsqrt(power / DT + EPSILON)[:, None]
    target = target.astype(BF16).astype(F32)

    inputs = student_input.astype(F32)
    error = loss_mask.astype(F32)[:, None] * (inputs + product - target)
    error_b = error.astype(BF16)

    inner = jnp.sum(error_b.astype(F32) * product, axis=1) / inv_scale
    slope = inv_scale**3 * inner / DS
    gains = [jnp.sum(v[256:259].astype(F32), axis=0) for v in rows]

    def outer(k):
        return lax.dot_general(
            features[k], error_b, (((0,), (0,)), ((), ())), preferred_element_type=F32
        )

    near, far = [swap_core(outer(k).astype(BF16)).astype(F32) for k in (4, 5)]
    shares = [
        outer(0) + far[:1024],
        outer(1) + near[:1024],
        outer(2) + near[1024:],
        outer(3) + far[1024:],
    ]

    sides = ((slice(0, 256), 1, 2), (slice(256, 512), 2, 1))
    carried = [
        jnp.concatenate([shares[a][:, cut], shares[3][:, cut]], axis=0).astype(BF16)
        for cut, a, _ in sides
    ]
    landed = [swap_x(v, HOPS[a]) for v, (_, a, _) in zip(carried, sides)]

    def piece(j, begin):
        end = begin + 1024
        value = dot_t(error_b, ordered[j][begin:end])
        value = value * inv_scale[:, None] * gains[j][begin:end]
        return (value - rows[j][:256, begin:end].astype(F32) * slope[:, None]).astype(BF16)

    def total(a, b):
        return (a.astype(F32) + b.astype(F32)).astype(BF16)

    first = [piece(0, 3072), piece(1, 3072)]
    second = after([piece(0, 2048), piece(1, 2048)], *carried)
    high = [piece(0, 1024), piece(1, 1024)]
    low = [piece(0, 0), piece(1, 0)]
    first = [swap_zy(first[j], j, 0) for j in range(2)]
    second = [swap_zy(second[j], j, 0) for j in range(2)]
    send = [total(high[j], first[j]) for j in range(2)]
    recv = [swap_zy(send[j], j, 1) for j in range(2)]
    keep = [total(low[j], second[j]) for j in range(2)]
    for step in (2, 3):
        width = 2048 >> step
        send = [total(keep[j][:, width:], recv[j][:, width:]) for j in range(2)]
        if step == 3:
            send[0] = after([send[0]], *landed)[0]
        keep = [total(keep[j][:, :width], recv[j][:, :width]) for j in range(2)]
        recv = [swap_zy(send[j], j, step) for j in range(2)]
    back = [keep[j].astype(F32) + recv[j].astype(F32) for j in range(2)]
    input_grad = error + jnp.concatenate(back, axis=1)

    ends = []
    for value, (cut, a, b) in zip(landed, sides):
        value = value.astype(F32)
        last = swap_x((shares[b][:, cut] + value[1024:]).astype(BF16), HOPS[b])
        ends.append(shares[0][:, cut] + value[:1024] + last.astype(F32))
    weight_grad = jnp.concatenate(ends, axis=1)
    return (weight_grad, input_grad.astype(BF16))


def solution(mesh):
    fine = Mesh(mesh.devices.reshape(2, 4, 4, 2, 2), ("section", "z", "y", "xhi", "core"))
    d, t = ("section", "xhi", "core"), ("z", "y")
    in_specs = (P(d, t), P(t, d), P(d), P(d, t), P(d, t), P(t), P(None, t), P(d))
    out_specs = (P(d, t), P(d, t))
    return jax.shard_map(
        on_device, mesh=fine, in_specs=in_specs, out_specs=out_specs, check_vma=False
    )
```

```python
import jax
import jax.numpy as jnp
from jax import lax
from jax.experimental import pallas as pl
from jax.experimental.pallas import tpu as pltpu
from jax.sharding import Mesh, PartitionSpec as P

DT = 16384
DS = 8192
EPSILON = 1e-05
F32 = jnp.float32
BF16 = jnp.bfloat16

X = ("section", "xhi")
ZYC = ("z", "y", "core")
HOPS = (0, 2, 3, 1)
FLIP = ((1, 0), (0, 1), (3, 0), (0, 3))
ANYWHERE = pl.BlockSpec(memory_space=pl.ANY)


def dot(a, b):
    return jnp.dot(a, b, preferred_element_type=F32)


def dot_t(a, b):
    return lax.dot_general(a, b, (((1,), (1,)), ((), ())), preferred_element_type=F32)


def first_of(j, core, step):
    return (3 - core if j else core) + step


def swap_zy(value, j, step):
    perm = []
    for z in range(4):
        for y in range(4):
            for core in range(2):
                dz, dy = FLIP[first_of(j, core, step) % 4]
                perm.append(((z * 4 + y) * 2 + core, ((z ^ dz) * 4 + (y ^ dy)) * 2 + core))
    return lax.ppermute(value, ZYC, perm)


def swap_x(value, r):
    return lax.ppermute(value, X, [(j, j ^ r) for j in range(4)])


def swap_core(value):
    return lax.ppermute(value, "core", [(0, 1), (1, 0)])


def split3(value):
    high = value.astype(BF16)
    rest = value - high.astype(F32)
    mid = rest.astype(BF16)
    low = (rest - mid.astype(F32)).astype(BF16)
    return high, mid, low


def call(kernel, grid, scalars, ins, outs, deps=(), scratch=(), moved=0, flops=0):
    n, m = len(ins), len(outs)

    def body(where, *refs):
        kernel(where, *refs[:n], *refs[n + len(deps) :])

    result = pl.pallas_call(
        body,
        grid_spec=pltpu.PrefetchScalarGridSpec(
            num_scalar_prefetch=1,
            grid=(grid,),
            in_specs=[pl.BlockSpec(b, i) for _, b, i in ins] + [ANYWHERE] * len(deps),
            out_specs=[pl.BlockSpec(b, i) for _, b, i in outs],
            scratch_shapes=list(scratch),
        ),
        out_shape=[s for s, _, _ in outs],
        compiler_params=pltpu.CompilerParams(vmem_limit_bytes=16 << 20),
        cost_estimate=pl.CostEstimate(flops=flops, bytes_accessed=moved, transcendentals=0),
    )(scalars, *[a for a, _, _ in ins], *deps)
    return result


def shape(dims, dtype):
    return jax.ShapeDtypeStruct(dims, dtype)


def nothing(*refs):
    pass


def after(values, *deps):
    n = len(values)
    return pl.pallas_call(
        nothing,
        in_specs=[ANYWHERE] * (n + len(deps)),
        out_specs=[ANYWHERE] * n,
        out_shape=[shape(v.shape, v.dtype) for v in values],
        input_output_aliases={i: i for i in range(n)},
        cost_estimate=pl.CostEstimate(flops=0, bytes_accessed=0, transcendentals=0),
    )(*values, *deps)


def block_of(t, where, j):
    gz, gy = (t >> 2) ^ where[0], (t & 3) ^ where[1]
    r = 0
    for step in range(4):
        d = first_of(j, where[2], step) & 3
        g = jnp.where(d & 1 == 0, gz, gy)
        gray = jnp.where(d & 2 == 0, (g ^ (g >> 1)) & 1, g >> 1)
        r = r | (gray << (3 - step))
    return r


def order_columns(proj, where):
    def kernel(where, a, b, out_a, out_b):
        out_a[...] = a[...]
        out_b[...] = b[...]

    return call(
        kernel,
        16,
        where,
        [(proj, (1024, 128), lambda r, w, j=j: (0, r ^ w[4 + j])) for j in range(2)],
        [(shape((1024, 2048), BF16), (1024, 128), lambda r, w: (0, r)) for j in range(2)],
        moved=4 * proj.size * 2,
    )


def order_projector(projector, gain, where, deps):
    def kernel(where, a, b, gain_a, gain_b, out_a, out_b):
        out_a[...] = (a[...].astype(F32) * gain_a[...]).astype(BF16)
        out_b[...] = (b[...].astype(F32) * gain_b[...]).astype(BF16)

    gain = gain[:, None]
    return call(
        kernel,
        16,
        where,
        [(projector, (128, 512), lambda r, w, j=j: (r ^ w[4 + j], 0)) for j in range(2)]
        + [(gain, (128, 1), lambda r, w, j=j: (r ^ w[4 + j], 0)) for j in range(2)],
        [(shape((2048, 512), BF16), (128, 512), lambda r, w: (r, 0)) for j in range(2)],
        deps=deps,
        moved=4 * projector.size * 2,
    )


def tensor_of(g, where):
    k = g >> 1
    hop = jnp.where(k < 2, 0, jnp.where(k < 4, 4, jnp.where(k < 6, 6, 2)))
    return (((where[3] * 2 + where[2]) ^ (hop | (k & 1))) << 1) | (g & 1)


def visit(*begins):
    def block(g):
        total = jnp.clip(g - begins[0], 0, 1)
        for begin in begins[1:]:
            total += jnp.clip(g - begin + 1, 0, 2)
        return total

    return block


PARTS = [(1024, visit(4 * h)) for h in range(4)] + [(2048, visit(6, 10)), (2048, visit(2, 14))]
PLACE = (0, 5, 1, 4, 2, 4, 3, 5)


def norm_rows(rows, inv_scale, where, deps):
    def kernel(where, scale, *refs):
        g = pl.program_id(0)
        outs = refs[2:]
        for k in range(8):

            @pl.when((g >> 1) == k)
            def _(k=k):
                out = outs[PLACE[k]]
                for j in range(2):
                    value = refs[j][...].astype(F32)
                    gain = value[256:257] + value[257:258] + value[258:259]
                    out[:, j * 256 : (j + 1) * 256] = (
                        value[:256] * scale[...] * gain
                    ).astype(BF16)

    return call(
        kernel,
        16,
        where,
        [(inv_scale[:, None], (256, 1), lambda g, w: (0, 0))]
        + [
            (rows[j], (272, 256), lambda g, w, j=j: (0, block_of(tensor_of(g, w), w, j)))
            for j in range(2)
        ],
        [
            (shape((256, width), BF16), (256, 512), lambda g, w, f=f: (0, f(g)))
            for width, f in PARTS
        ],
        deps=deps,
        moved=4 * 272 * 4096 * 2,
    )


def forward(features, weight, where, deps):
    def kernel(where, *refs):
        weight, out, out_a, out_b = refs[6:]
        g = pl.program_id(0)

        @pl.when(g == 0)
        def _():
            out[...] = jnp.zeros_like(out)

        for k in range(8):

            @pl.when((g >> 1) == k)
            def _(k=k):
                out[...] += dot(refs[PLACE[k]][...], weight[...])

        out_a[...] = weight[:256, :]
        out_b[...] = weight[256:, :]

    return call(
        kernel,
        16,
        where,
        [
            (v, (256, 512), lambda g, w, f=f: (0, f(g)))
            for v, (_, f) in zip(features, PARTS)
        ]
        + [(weight, (512, 512), lambda g, w: (tensor_of(g, w), 0))],
        [(shape((256, 512), F32), (256, 512), lambda g, w: (0, 0))]
        + [
            (
                shape((4096, 512), BF16),
                (256, 512),
                lambda g, w, j=j: (block_of(tensor_of(g, w), w, j), 0),
            )
            for j in range(2)
        ],
        deps=deps,
        moved=2 * weight.size * 2 + 256 * 8192 * 2,
        flops=2 * 256 * 8192 * 512,
    )


def squares(value):
    value = value.astype(F32)
    value = value * value
    return value[:, :128] + value[:, 128:256] + value[:, 256:384] + value[:, 384:]


def row_block(g):
    return jnp.where(g < 2, 2 * g + 1, 2 * g - 4)


def project(pieces, projector, where, deps):
    def kernel(where, a, b, c, projector, out, out_squares):
        acc = dot(a[...], projector[0:512, :])
        acc += dot(b[...], projector[512:1024, :])
        out[...] = acc + dot(c[...], projector[1024:1536, :])
        out_squares[...] = squares(a[...]) + squares(b[...]) + squares(c[...])

    return call(
        kernel,
        4,
        where,
        [(p, (256, 512), lambda g, w: (g, 0)) for p in pieces]
        + [(projector, (2048, 512), lambda g, w: (0, 0))],
        [
            (shape((1024, 512), F32), (256, 512), lambda g, w: (g, 0)),
            (shape((1024, 128), F32), (256, 128), lambda g, w: (g, 0)),
        ],
        deps=deps,
        moved=10 << 20,
        flops=2 * 1024 * 1536 * 512,
    )


def packed_extra(power):
    high, mid, low = split3(power)
    column = lax.broadcasted_iota(jnp.int32, (power.shape[0], 128), 1)
    zero = jnp.zeros((), F32)
    high, mid, low = high.astype(F32), mid.astype(F32), low.astype(F32)
    extra = jnp.where(column == 0, high, jnp.where(column == 1, mid, jnp.where(column == 2, low, zero)))
    return extra.astype(BF16)


def project_last(piece, projector, acc, acc_squares, where, deps):
    def kernel(where, piece, projector, acc, acc_squares, out_send, out_keep):
        g = pl.program_id(0)
        total = acc[...] + dot(piece[...], projector[...])
        power = jnp.sum(acc_squares[...] + squares(piece[...]), axis=1, keepdims=True)

        @pl.when(g < 2)
        def _():
            out_send[:, :512] = total.astype(BF16)
            out_send[:, 512:] = packed_extra(power)

        @pl.when(g >= 2)
        def _():
            out_keep[:, :512] = total
            out_keep[:, 512:] = jnp.broadcast_to(power, (256, 128))

    return call(
        kernel,
        4,
        where,
        [
            (piece, (256, 512), lambda g, w: (row_block(g), 0)),
            (projector, (512, 512), lambda g, w: (3, 0)),
            (acc, (256, 512), lambda g, w: (row_block(g), 0)),
            (acc_squares, (256, 128), lambda g, w: (row_block(g), 0)),
        ],
        [
            (shape((512, 640), BF16), (256, 640), lambda g, w: (jnp.minimum(g, 1), 0)),
            (shape((512, 640), F32), (256, 640), lambda g, w: (jnp.maximum(g - 2, 0), 0)),
        ],
        deps=deps,
        moved=6 << 20,
        flops=2 * 1024 * 512 * 512,
    )


def add_pair(keep, recv, k, packed, where):
    def kernel(where, keep, recv, out):
        total = keep[:, :512] + recv[:, :512].astype(F32)
        power = keep[:, 512:513] + jnp.sum(recv[:, 512:].astype(F32), axis=1, keepdims=True)
        out[:, :512] = total.astype(out.dtype)
        if packed:
            out[:, 512:] = packed_extra(power)
        else:
            out[:, 512:] = jnp.broadcast_to(power, (256, 128))

    return call(
        kernel,
        1,
        where,
        [(v, (256, 640), lambda g, w: (k, 0)) for v in (keep, recv)],
        [(shape((256, 640), BF16 if packed else F32), (256, 640), lambda g, w: (0, 0))],
        moved=2 << 20,
    )[0]


def on_device(
    teacher_input,
    teacher_proj,
    teacher_gain,
    projector,
    student_input,
    student_gain,
    student_weight,
    loss_mask,
):
    core = lax.axis_index("core")
    z, y = lax.axis_index("z"), lax.axis_index("y")
    chip = lax.axis_index(X)

    def address(j):
        total = 0
        for step in range(4):
            d = first_of(j, core, step) & 3
            g = jnp.where(d & 1 == 0, z, y)
            bit = jnp.where(d & 2 == 0, (g ^ (g >> 1)) & 1, g >> 1)
            total = total | (bit << (3 - step))
        return total

    where = jnp.stack([z, y, core, chip, address(0), address(1)]).astype(jnp.int32)

    high, mid, low = split3(student_gain)
    packed = jnp.concatenate(
        [student_input, jnp.stack([high, mid, low]), jnp.zeros((13, 512), BF16)], axis=0
    )
    rows = []
    for j in range(2):
        mine = packed[:, j * 256 : (j + 1) * 256]
        for step in (3, 2, 1, 0):
            mine = jnp.concatenate([mine, swap_zy(mine, j, step)], axis=1)
        rows.append(mine)

    own = [teacher_input] + [swap_x(teacher_input, h) for h in HOPS[1:]]
    own = [[a, swap_core(a)] for a in own]
    streams = [jnp.concatenate(own[2 * j] + own[2 * j + 1], axis=0) for j in range(2)]

    proj = order_columns(teacher_proj, where)

    sent, kept = [], []
    for j in range(2):

        def part(begin, j=j):
            return dot(streams[j], proj[j][:, begin : begin + 512]).astype(BF16)

        sent.append((part(1536), part(1024)))
        kept.append((part(512), part(0)))
    scaled = order_projector(projector, teacher_gain, where, (kept[1][1],))

    power_s = sum(jnp.sum(jnp.square(v[:256].astype(F32)), axis=1) for v in rows)
    inv_scale = lax.rsqrt(power_s / DS + EPSILON)
    features = norm_rows(rows, inv_scale, where, (kept[0][1], kept[1][1]))

    hidden = []
    for j in range(2):
        first, second = swap_zy(sent[j][0], j, 0), swap_zy(sent[j][1], j, 0)
        send = (kept[j][0].astype(F32) + first.astype(F32)).astype(BF16)
        keep = (kept[j][1].astype(F32) + second.astype(F32)).astype(BF16)
        if j == 0:
            (send,) = after([send], *rows)
        recv = swap_zy(send, j, 1)
        send = (keep[:, 256:].astype(F32) + recv[:, 256:].astype(F32)).astype(BF16)
        keep = (keep[:, :256].astype(F32) + recv[:, :256].astype(F32)).astype(BF16)
        recv = swap_zy(send, j, 2)
        keep = (keep.astype(F32) + recv.astype(F32)).astype(BF16)
        recv = swap_zy(keep, j, 3)
        recv = jnp.concatenate([recv[:, 128:], recv[:, :128]], axis=1)
        hidden.append((keep.astype(F32) + recv.astype(F32)).astype(BF16))

    pieces = []
    for j in range(2):
        mine = jnp.concatenate([hidden[j], swap_zy(hidden[j], j, 2)], axis=1)
        other = swap_zy(mine, j, 1)
        pieces.append([mine, other, swap_zy(mine, j, 0), swap_zy(other, j, 0)])

    sums, parts = [], []
    begun = [
        project(pieces[j][:3], scaled[j], where, (features[0],) if j == 0 else ())
        for j in range(2)
    ]
    for j in (1, 0):
        deps = (begun[0][0],) if j else ()
        send, keep = project_last(pieces[j][3], scaled[j], *begun[j], where, deps)
        recv = swap_core(send)
        for k in range(2):
            hop = HOPS[2 * j + k]
            part = add_pair(keep, recv, k, bool(hop), where)
            parts.append(part)
            sums.append(swap_x(part, hop) if hop else part)
    own = sums.pop(2)
    sums = [own] + sums
    product, *ordered = forward(features, student_weight, where, parts)
    target = sum(s[:, :512].astype(F32) for s in sums)
    power = sums[0][:, 512] + sum(jnp.sum(s[:, 512:].astype(F32), axis=1) for s in sums[1:])
    target = target * lax.rsqrt(power / DT + EPSILON)[:, None]
    target = target.astype(BF16).astype(F32)

    inputs = student_input.astype(F32)
    error = loss_mask.astype(F32)[:, None] * (inputs + product - target)
    error_b = error.astype(BF16)

    inner = jnp.sum(error_b.astype(F32) * product, axis=1) / inv_scale
    slope = inv_scale**3 * inner / DS
    gains = [jnp.sum(v[256:259].astype(F32), axis=0) for v in rows]

    def outer(k):
        return lax.dot_general(
            features[k], error_b, (((0,), (0,)), ((), ())), preferred_element_type=F32
        )

    near, far = [swap_core(outer(k).astype(BF16)).astype(F32) for k in (4, 5)]
    shares = [
        outer(0) + far[:1024],
        outer(1) + near[:1024],
        outer(2) + near[1024:],
        outer(3) + far[1024:],
    ]

    sides = ((slice(0, 256), 1, 2), (slice(256, 512), 2, 1))
    carried = [
        jnp.concatenate([shares[a][:, cut], shares[3][:, cut]], axis=0).astype(BF16)
        for cut, a, _ in sides
    ]
    landed = [swap_x(v, HOPS[a]) for v, (_, a, _) in zip(carried, sides)]

    def piece(j, begin):
        end = begin + 1024
        value = dot_t(error_b, ordered[j][begin:end])
        value = value * inv_scale[:, None] * gains[j][begin:end]
        return (value - rows[j][:256, begin:end].astype(F32) * slope[:, None]).astype(BF16)

    def total(a, b):
        return (a.astype(F32) + b.astype(F32)).astype(BF16)

    first = [piece(0, 3072), piece(1, 3072)]
    second = after([piece(0, 2048), piece(1, 2048)], *carried)
    high = [piece(0, 1024), piece(1, 1024)]
    low = [piece(0, 0), piece(1, 0)]
    first = [swap_zy(first[j], j, 0) for j in range(2)]
    second = [swap_zy(second[j], j, 0) for j in range(2)]
    send = [total(high[j], first[j]) for j in range(2)]
    recv = [swap_zy(send[j], j, 1) for j in range(2)]
    keep = [total(low[j], second[j]) for j in range(2)]
    for step in (2, 3):
        width = 2048 >> step
        send = [total(keep[j][:, width:], recv[j][:, width:]) for j in range(2)]
        if step == 3:
            send[0] = after([send[0]], *landed)[0]
        keep = [total(keep[j][:, :width], recv[j][:, :width]) for j in range(2)]
        recv = [swap_zy(send[j], j, step) for j in range(2)]
    back = [keep[j].astype(F32) + recv[j].astype(F32) for j in range(2)]
    input_grad = error + jnp.concatenate(back, axis=1)

    ends = []
    for value, (cut, a, b) in zip(landed, sides):
        value = value.astype(F32)
        last = swap_x((shares[b][:, cut] + value[1024:]).astype(BF16), HOPS[b])
        ends.append(shares[0][:, cut] + value[:1024] + last.astype(F32))
    weight_grad = jnp.concatenate(ends, axis=1)
    return (weight_grad, input_grad.astype(BF16))


def solution(mesh):
    fine = Mesh(mesh.devices.reshape(2, 4, 4, 2, 2), ("section", "z", "y", "xhi", "core"))
    d, t = ("section", "xhi", "core"), ("z", "y")
    in_specs = (P(d, t), P(t, d), P(d), P(d, t), P(d, t), P(t), P(None, t), P(d))
    out_specs = (P(d, t), P(d, t))
    return jax.shard_map(
        on_device, mesh=fine, in_specs=in_specs, out_specs=out_specs, check_vma=False
    )
```

```python
import jax
import jax.numpy as jnp
from jax import lax
from jax.experimental import pallas as pl
from jax.experimental.pallas import tpu as pltpu
from jax.sharding import Mesh, PartitionSpec as P

DT = 16384
DS = 8192
EPSILON = 1e-05
F32 = jnp.float32
BF16 = jnp.bfloat16

X = ("section", "xhi")
ZYC = ("z", "y", "core")
HOPS = (0, 2, 3, 1)
FLIP = ((1, 0), (0, 1), (3, 0), (0, 3))
ANYWHERE = pl.BlockSpec(memory_space=pl.ANY)


def dot(a, b):
    return jnp.dot(a, b, preferred_element_type=F32)


def dot_t(a, b):
    return lax.dot_general(a, b, (((1,), (1,)), ((), ())), preferred_element_type=F32)


def first_of(j, core, step):
    return (3 - core if j else core) + step


def swap_zy(value, j, step):
    perm = []
    for z in range(4):
        for y in range(4):
            for core in range(2):
                dz, dy = FLIP[first_of(j, core, step) % 4]
                perm.append(((z * 4 + y) * 2 + core, ((z ^ dz) * 4 + (y ^ dy)) * 2 + core))
    return lax.ppermute(value, ZYC, perm)


def swap_x(value, r):
    return lax.ppermute(value, X, [(j, j ^ r) for j in range(4)])


def swap_core(value):
    return lax.ppermute(value, "core", [(0, 1), (1, 0)])


def split3(value):
    high = value.astype(BF16)
    rest = value - high.astype(F32)
    mid = rest.astype(BF16)
    low = (rest - mid.astype(F32)).astype(BF16)
    return high, mid, low


def call(kernel, grid, scalars, ins, outs, deps=(), scratch=(), moved=0, flops=0):
    n, m = len(ins), len(outs)

    def body(where, *refs):
        kernel(where, *refs[:n], *refs[n + len(deps) :])

    result = pl.pallas_call(
        body,
        grid_spec=pltpu.PrefetchScalarGridSpec(
            num_scalar_prefetch=1,
            grid=(grid,),
            in_specs=[pl.BlockSpec(b, i) for _, b, i in ins] + [ANYWHERE] * len(deps),
            out_specs=[pl.BlockSpec(b, i) for _, b, i in outs],
            scratch_shapes=list(scratch),
        ),
        out_shape=[s for s, _, _ in outs],
        compiler_params=pltpu.CompilerParams(vmem_limit_bytes=16 << 20),
        cost_estimate=pl.CostEstimate(flops=flops, bytes_accessed=moved, transcendentals=0),
    )(scalars, *[a for a, _, _ in ins], *deps)
    return result


def shape(dims, dtype):
    return jax.ShapeDtypeStruct(dims, dtype)


def nothing(*refs):
    pass


def after(values, *deps):
    n = len(values)
    return pl.pallas_call(
        nothing,
        in_specs=[ANYWHERE] * (n + len(deps)),
        out_specs=[ANYWHERE] * n,
        out_shape=[shape(v.shape, v.dtype) for v in values],
        input_output_aliases={i: i for i in range(n)},
        cost_estimate=pl.CostEstimate(flops=0, bytes_accessed=0, transcendentals=0),
    )(*values, *deps)


def block_of(t, where, j):
    gz, gy = (t >> 2) ^ where[0], (t & 3) ^ where[1]
    r = 0
    for step in range(4):
        d = first_of(j, where[2], step) & 3
        g = jnp.where(d & 1 == 0, gz, gy)
        gray = jnp.where(d & 2 == 0, (g ^ (g >> 1)) & 1, g >> 1)
        r = r | (gray << (3 - step))
    return r


def order_columns(proj, where):
    def kernel(where, a, b, out_a, out_b):
        out_a[...] = a[...]
        out_b[...] = b[...]

    return call(
        kernel,
        16,
        where,
        [(proj, (1024, 128), lambda r, w, j=j: (0, r ^ w[4 + j])) for j in range(2)],
        [(shape((1024, 2048), BF16), (1024, 128), lambda r, w: (0, r)) for j in range(2)],
        moved=4 * proj.size * 2,
    )


def order_projector(projector, gain, where, deps):
    def kernel(where, a, b, gain_a, gain_b, out_a, out_b):
        out_a[...] = (a[...].astype(F32) * gain_a[...]).astype(BF16)
        out_b[...] = (b[...].astype(F32) * gain_b[...]).astype(BF16)

    gain = gain[:, None]
    return call(
        kernel,
        16,
        where,
        [(projector, (128, 512), lambda r, w, j=j: (r ^ w[4 + j], 0)) for j in range(2)]
        + [(gain, (128, 1), lambda r, w, j=j: (r ^ w[4 + j], 0)) for j in range(2)],
        [(shape((2048, 512), BF16), (128, 512), lambda r, w: (r, 0)) for j in range(2)],
        deps=deps,
        moved=4 * projector.size * 2,
    )


def tensor_of(g, where):
    k = g >> 1
    hop = jnp.where(k < 2, 0, jnp.where(k < 4, 4, jnp.where(k < 6, 6, 2)))
    return (((where[3] * 2 + where[2]) ^ (hop | (k & 1))) << 1) | (g & 1)


def visit(*begins):
    def block(g):
        total = jnp.clip(g - begins[0], 0, 1)
        for begin in begins[1:]:
            total += jnp.clip(g - begin + 1, 0, 2)
        return total

    return block


PARTS = [(1024, visit(4 * h)) for h in range(4)] + [(2048, visit(6, 10)), (2048, visit(2, 14))]
PLACE = (0, 5, 1, 4, 2, 4, 3, 5)


def norm_rows(rows, inv_scale, where, deps):
    def kernel(where, scale, *refs):
        g = pl.program_id(0)
        outs = refs[2:]
        for k in range(8):

            @pl.when((g >> 1) == k)
            def _(k=k):
                out = outs[PLACE[k]]
                for j in range(2):
                    value = refs[j][...].astype(F32)
                    gain = value[256:257] + value[257:258] + value[258:259]
                    out[:, j * 256 : (j + 1) * 256] = (
                        value[:256] * scale[...] * gain
                    ).astype(BF16)

    return call(
        kernel,
        16,
        where,
        [(inv_scale[:, None], (256, 1), lambda g, w: (0, 0))]
        + [
            (rows[j], (272, 256), lambda g, w, j=j: (0, block_of(tensor_of(g, w), w, j)))
            for j in range(2)
        ],
        [
            (shape((256, width), BF16), (256, 512), lambda g, w, f=f: (0, f(g)))
            for width, f in PARTS
        ],
        deps=deps,
        moved=4 * 272 * 4096 * 2,
    )


def forward(features, weight, where, deps):
    def kernel(where, *refs):
        weight, out, out_a, out_b = refs[6:]
        g = pl.program_id(0)

        @pl.when(g == 0)
        def _():
            out[...] = jnp.zeros_like(out)

        for k in range(8):

            @pl.when((g >> 1) == k)
            def _(k=k):
                out[...] += dot(refs[PLACE[k]][...], weight[...])

        out_a[...] = weight[:256, :]
        out_b[...] = weight[256:, :]

    return call(
        kernel,
        16,
        where,
        [
            (v, (256, 512), lambda g, w, f=f: (0, f(g)))
            for v, (_, f) in zip(features, PARTS)
        ]
        + [(weight, (512, 512), lambda g, w: (tensor_of(g, w), 0))],
        [(shape((256, 512), F32), (256, 512), lambda g, w: (0, 0))]
        + [
            (
                shape((4096, 512), BF16),
                (256, 512),
                lambda g, w, j=j: (block_of(tensor_of(g, w), w, j), 0),
            )
            for j in range(2)
        ],
        deps=deps,
        moved=2 * weight.size * 2 + 256 * 8192 * 2,
        flops=2 * 256 * 8192 * 512,
    )


def squares(value):
    value = value.astype(F32)
    value = value * value
    return value[:, :128] + value[:, 128:256] + value[:, 256:384] + value[:, 384:]


def row_block(g):
    return jnp.where(g < 2, 2 * g + 1, 2 * g - 4)


def project(pieces, projector, where, deps):
    def kernel(where, a, b, c, projector, out, out_squares):
        acc = dot(a[...], projector[0:512, :])
        acc += dot(b[...], projector[512:1024, :])
        out[...] = acc + dot(c[...], projector[1024:1536, :])
        out_squares[...] = squares(a[...]) + squares(b[...]) + squares(c[...])

    return call(
        kernel,
        4,
        where,
        [(p, (256, 512), lambda g, w: (g, 0)) for p in pieces]
        + [(projector, (2048, 512), lambda g, w: (0, 0))],
        [
            (shape((1024, 512), F32), (256, 512), lambda g, w: (g, 0)),
            (shape((1024, 128), F32), (256, 128), lambda g, w: (g, 0)),
        ],
        deps=deps,
        moved=10 << 20,
        flops=2 * 1024 * 1536 * 512,
    )


def packed_extra(power):
    high, mid, low = split3(power)
    column = lax.broadcasted_iota(jnp.int32, (power.shape[0], 128), 1)
    zero = jnp.zeros((), F32)
    high, mid, low = high.astype(F32), mid.astype(F32), low.astype(F32)
    extra = jnp.where(column == 0, high, jnp.where(column == 1, mid, jnp.where(column == 2, low, zero)))
    return extra.astype(BF16)


def project_last(piece, projector, acc, acc_squares, where, deps):
    def kernel(where, piece, projector, acc, acc_squares, out_send, out_keep):
        g = pl.program_id(0)
        total = acc[...] + dot(piece[...], projector[...])
        power = jnp.sum(acc_squares[...] + squares(piece[...]), axis=1, keepdims=True)

        @pl.when(g < 2)
        def _():
            out_send[:, :512] = total.astype(BF16)
            out_send[:, 512:] = packed_extra(power)

        @pl.when(g >= 2)
        def _():
            out_keep[:, :512] = total
            out_keep[:, 512:] = jnp.broadcast_to(power, (256, 128))

    return call(
        kernel,
        4,
        where,
        [
            (piece, (256, 512), lambda g, w: (row_block(g), 0)),
            (projector, (512, 512), lambda g, w: (3, 0)),
            (acc, (256, 512), lambda g, w: (row_block(g), 0)),
            (acc_squares, (256, 128), lambda g, w: (row_block(g), 0)),
        ],
        [
            (shape((512, 640), BF16), (256, 640), lambda g, w: (jnp.minimum(g, 1), 0)),
            (shape((512, 640), F32), (256, 640), lambda g, w: (jnp.maximum(g - 2, 0), 0)),
        ],
        deps=deps,
        moved=6 << 20,
        flops=2 * 1024 * 512 * 512,
    )


def add_pair(keep, recv, k, packed, where):
    def kernel(where, keep, recv, out):
        total = keep[:, :512] + recv[:, :512].astype(F32)
        power = keep[:, 512:513] + jnp.sum(recv[:, 512:].astype(F32), axis=1, keepdims=True)
        out[:, :512] = total.astype(out.dtype)
        if packed:
            out[:, 512:] = packed_extra(power)
        else:
            out[:, 512:] = jnp.broadcast_to(power, (256, 128))

    return call(
        kernel,
        1,
        where,
        [(v, (256, 640), lambda g, w: (k, 0)) for v in (keep, recv)],
        [(shape((256, 640), BF16 if packed else F32), (256, 640), lambda g, w: (0, 0))],
        moved=2 << 20,
    )[0]


def on_device(
    teacher_input,
    teacher_proj,
    teacher_gain,
    projector,
    student_input,
    student_gain,
    student_weight,
    loss_mask,
):
    core = lax.axis_index("core")
    z, y = lax.axis_index("z"), lax.axis_index("y")
    chip = lax.axis_index(X)

    def address(j):
        total = 0
        for step in range(4):
            d = first_of(j, core, step) & 3
            g = jnp.where(d & 1 == 0, z, y)
            bit = jnp.where(d & 2 == 0, (g ^ (g >> 1)) & 1, g >> 1)
            total = total | (bit << (3 - step))
        return total

    where = jnp.stack([z, y, core, chip, address(0), address(1)]).astype(jnp.int32)

    high, mid, low = split3(student_gain)
    packed = jnp.concatenate(
        [student_input, jnp.stack([high, mid, low]), jnp.zeros((13, 512), BF16)], axis=0
    )
    rows = []
    for j in range(2):
        mine = packed[:, j * 256 : (j + 1) * 256]
        for step in (3, 2, 1, 0):
            mine = jnp.concatenate([mine, swap_zy(mine, j, step)], axis=1)
        rows.append(mine)

    own = [teacher_input] + [swap_x(teacher_input, h) for h in HOPS[1:]]
    own = [[a, swap_core(a)] for a in own]
    streams = [jnp.concatenate(own[2 * j] + own[2 * j + 1], axis=0) for j in range(2)]

    proj = order_columns(teacher_proj, where)

    sent, kept = [], []
    for j in range(2):

        def part(begin, j=j):
            return dot(streams[j], proj[j][:, begin : begin + 512]).astype(BF16)

        sent.append((part(1536), part(1024)))
        kept.append((part(512), part(0)))
    scaled = order_projector(projector, teacher_gain, where, (kept[1][1],))

    power_s = sum(jnp.sum(jnp.square(v[:256].astype(F32)), axis=1) for v in rows)
    inv_scale = lax.rsqrt(power_s / DS + EPSILON)
    features = norm_rows(rows, inv_scale, where, (kept[0][1], kept[1][1]))

    hidden = []
    for j in range(2):
        first, second = swap_zy(sent[j][0], j, 0), swap_zy(sent[j][1], j, 0)
        send = (kept[j][0].astype(F32) + first.astype(F32)).astype(BF16)
        keep = (kept[j][1].astype(F32) + second.astype(F32)).astype(BF16)
        recv = swap_zy(send, j, 1)
        send = (keep[:, 256:].astype(F32) + recv[:, 256:].astype(F32)).astype(BF16)
        keep = (keep[:, :256].astype(F32) + recv[:, :256].astype(F32)).astype(BF16)
        if j == 0:
            (send,) = after([send], *rows)
        recv = swap_zy(send, j, 2)
        keep = (keep.astype(F32) + recv.astype(F32)).astype(BF16)
        recv = swap_zy(keep, j, 3)
        recv = jnp.concatenate([recv[:, 128:], recv[:, :128]], axis=1)
        hidden.append((keep.astype(F32) + recv.astype(F32)).astype(BF16))

    pieces = []
    for j in range(2):
        mine = jnp.concatenate([hidden[j], swap_zy(hidden[j], j, 2)], axis=1)
        other = swap_zy(mine, j, 1)
        pieces.append([mine, other, swap_zy(mine, j, 0), swap_zy(other, j, 0)])

    sums, parts = [], []
    begun = [
        project(pieces[j][:3], scaled[j], where, (features[0],) if j == 0 else ())
        for j in range(2)
    ]
    for j in (1, 0):
        deps = (begun[0][0],) if j else ()
        send, keep = project_last(pieces[j][3], scaled[j], *begun[j], where, deps)
        recv = swap_core(send)
        for k in range(2):
            hop = HOPS[2 * j + k]
            part = add_pair(keep, recv, k, bool(hop), where)
            parts.append(part)
            sums.append(swap_x(part, hop) if hop else part)
    own = sums.pop(2)
    sums = [own] + sums
    product, *ordered = forward(features, student_weight, where, parts)
    target = sum(s[:, :512].astype(F32) for s in sums)
    power = sums[0][:, 512] + sum(jnp.sum(s[:, 512:].astype(F32), axis=1) for s in sums[1:])
    target = target * lax.rsqrt(power / DT + EPSILON)[:, None]
    target = target.astype(BF16).astype(F32)

    inputs = student_input.astype(F32)
    error = loss_mask.astype(F32)[:, None] * (inputs + product - target)
    error_b = error.astype(BF16)

    inner = jnp.sum(error_b.astype(F32) * product, axis=1) / inv_scale
    slope = inv_scale**3 * inner / DS
    gains = [jnp.sum(v[256:259].astype(F32), axis=0) for v in rows]

    def outer(k):
        return lax.dot_general(
            features[k], error_b, (((0,), (0,)), ((), ())), preferred_element_type=F32
        )

    near, far = [swap_core(outer(k).astype(BF16)).astype(F32) for k in (4, 5)]
    shares = [
        outer(0) + far[:1024],
        outer(1) + near[:1024],
        outer(2) + near[1024:],
        outer(3) + far[1024:],
    ]

    sides = ((slice(0, 256), 1, 2), (slice(256, 512), 2, 1))
    carried = [
        jnp.concatenate([shares[a][:, cut], shares[3][:, cut]], axis=0).astype(BF16)
        for cut, a, _ in sides
    ]
    landed = [swap_x(v, HOPS[a]) for v, (_, a, _) in zip(carried, sides)]

    def piece(j, begin):
        end = begin + 1024
        value = dot_t(error_b, ordered[j][begin:end])
        value = value * inv_scale[:, None] * gains[j][begin:end]
        return (value - rows[j][:256, begin:end].astype(F32) * slope[:, None]).astype(BF16)

    def total(a, b):
        return (a.astype(F32) + b.astype(F32)).astype(BF16)

    first = [piece(0, 3072), piece(1, 3072)]
    second = after([piece(0, 2048), piece(1, 2048)], *carried)
    high = [piece(0, 1024), piece(1, 1024)]
    low = [piece(0, 0), piece(1, 0)]
    first = [swap_zy(first[j], j, 0) for j in range(2)]
    second = [swap_zy(second[j], j, 0) for j in range(2)]
    send = [total(high[j], first[j]) for j in range(2)]
    recv = [swap_zy(send[j], j, 1) for j in range(2)]
    keep = [total(low[j], second[j]) for j in range(2)]
    for step in (2, 3):
        width = 2048 >> step
        send = [total(keep[j][:, width:], recv[j][:, width:]) for j in range(2)]
        if step == 3:
            send[0] = after([send[0]], *landed)[0]
        keep = [total(keep[j][:, :width], recv[j][:, :width]) for j in range(2)]
        recv = [swap_zy(send[j], j, step) for j in range(2)]
    back = [keep[j].astype(F32) + recv[j].astype(F32) for j in range(2)]
    input_grad = error + jnp.concatenate(back, axis=1)

    ends = []
    for value, (cut, a, b) in zip(landed, sides):
        value = value.astype(F32)
        last = swap_x((shares[b][:, cut] + value[1024:]).astype(BF16), HOPS[b])
        ends.append(shares[0][:, cut] + value[:1024] + last.astype(F32))
    weight_grad = jnp.concatenate(ends, axis=1)
    return (weight_grad, input_grad.astype(BF16))


def solution(mesh):
    fine = Mesh(mesh.devices.reshape(2, 4, 4, 2, 2), ("section", "z", "y", "xhi", "core"))
    d, t = ("section", "xhi", "core"), ("z", "y")
    in_specs = (P(d, t), P(t, d), P(d), P(d, t), P(d, t), P(t), P(None, t), P(d))
    out_specs = (P(d, t), P(d, t))
    return jax.shard_map(
        on_device, mesh=fine, in_specs=in_specs, out_specs=out_specs, check_vma=False
    )
```
